256 devices in a mesh: tile: 64 (over y, x, z_lo), agg: 4 (over z_hi, core).
Axes of the slice: x: 4, y: 4, z: 8 (z_hi: 2, z_lo: 4; z = z_hi * 4 + z_lo), core: 2. Of those that a mesh axis runs over, the one named last changes fastest.
Arguments:
- a_blocks: bfloat16 [4096, 6, 4096], P(('tile', 'agg')), may hold values from -0.75 to 0.75
- p_blocks: bfloat16 [4096, 4096], P(('tile', 'agg')), may hold values from -0.75 to 0.75
- columns: int32 [4096, 6], P(('tile', 'agg')), may hold values from 0 to 4095, as said below
- agg_ids: int32 [4096], replicated, may hold values from 0 to 1637, never falling along the last dimension, each value on 1 to 4 neighbouring positions
Outputs:
- coarse: bfloat16 [4096, 7, 4096], P('tile')
The draws below stay inside these ranges and needn't reach their ends.
Inputs may be any that keep to these rules, and one draw needn't show every extreme that they name: `columns`: each row's first entry is the row itself; the others are block rows other than itself within 3 of it, distinct except in the first and last 3 rows, where a column may be named twice. `agg_ids`: starts at 0, never falls, rises by at most 1 from row to row; each aggregate has 1 to 4 rows.
All inputs are finite; a program needn't handle non-finite values.
Results may differ from the reference program's by a relative error of at most 0.015.
Values may be sent and summed in bfloat16 or wider, within the bound.
A program may use at most 64 MiB of HBM per device.

```python
import math
import jax
import jax.numpy as jnp
import numpy as np
from jax import lax

BS = 64
NNZB = 6
REACH = 3
MOST = 4
BLK_DEV = 16
BAND = 7
NB = 4096
NAGG = 1638


def draw_columns(key, part):
    key = jax.random.fold_in(key, 11)
    count = NB
    scores = jax.random.randint(key, (count, 2 * REACH), 0, 1 << 20) * 8 + jnp.arange(2 * REACH, dtype=jnp.int32)
    order = jnp.argsort(scores, axis=1)
    moves = jnp.concatenate([jnp.arange(-REACH, 0, dtype=jnp.int32), jnp.arange(1, REACH + 1, dtype=jnp.int32)])
    chosen = moves[order[:, :NNZB - 1]]
    place = jnp.arange(count, dtype=jnp.int32)[:, None]
    target = place + chosen
    target = jnp.where((target < 0) | (target >= count), place - chosen, target)
    return jnp.concatenate([place, target], axis=1).astype(jnp.int32)


def block_levels(stream_key, extent, cuts, least, largest):
    gain, own = 1.0, jax.random.fold_in(stream_key, 6)
    for axis_at, blocks in cuts:
        draws = jnp.exp(jax.random.uniform(jax.random.fold_in(own, axis_at), (blocks,), jnp.float32, least / len(cuts), largest / len(cuts)))
        gain = gain * jnp.repeat(draws, extent[axis_at] // blocks).reshape([-1 if axis == axis_at else 1 for axis in range(len(extent))])
    return gain


def length_profile(amount, total, bound, skew):
    portions = [(1 << 20) // math.isqrt(rank ** skew) + 1 for rank in range(2, amount + 1)]
    surplus, holding = total - bound - (amount - 1), [1] * (amount - 1)
    while surplus > 0:
        movable = [i for i in range(amount - 1) if holding[i] < bound]
        pool, left = sum([portions[i] for i in movable]), surplus
        for i in movable:
            extra = min(bound - holding[i], max(1, left * portions[i] // pool), surplus)
            holding[i] = holding[i] + extra
            surplus = surplus - extra
    return np.array([bound] + holding)


def ragged(own_key, amount, total, bound, skew):
    if amount == 2:
        one = jax.random.randint(own_key, (), max(1, total - bound), min(bound, total - 1) + 1)
        return jnp.stack([one, total - one])
    sizes = jnp.asarray(length_profile(amount, total, bound, skew), jnp.int32)
    couples = (amount - 1) // 2
    source_of, receiver = sizes[1:1 + 2 * couples:2], sizes[2:2 + 2 * couples:2]
    slack = jnp.minimum(source_of - 1, bound - receiver)
    passed = jax.random.randint(jax.random.fold_in(own_key, 1), (couples,), 0, 1 << 20) % (slack + 1)
    sizes = sizes.at[1:1 + 2 * couples:2].set(source_of - passed).at[2:2 + 2 * couples:2].set(receiver + passed)
    return sizes[jax.random.permutation(jax.random.fold_in(own_key, 2), amount)]


def scatter_about(own_key, extent, scale, limit, pieces=(), held_as=jnp.bfloat16):
    values = scale * jax.random.normal(own_key, extent, jnp.float32)
    if pieces:
        values = values * block_levels(own_key, extent, pieces, -0.22, 0.18)
    return jnp.clip(values, -limit, limit).astype(held_as)


def setup_inputs(seed: int = 0) -> dict:
    key_list = jax.random.split(jax.random.key(seed), 5)
    a_blocks = scatter_about(key_list[0], (NB, NNZB, BS * BS), BS ** -0.5, 0.75, ((0, 256),))
    p_blocks = scatter_about(key_list[1], (NB, BS * BS), BS ** -0.5, 0.75, ((0, 256),))
    columns = draw_columns(jax.random.fold_in(key_list[4], 71), 0)
    agg_ids = jnp.searchsorted(jnp.cumsum(ragged(key_list[3], NAGG, NB, MOST, 2)), jnp.arange(NB), side="right").astype(jnp.int32)
    return {"a_blocks": a_blocks, "p_blocks": p_blocks, "columns": columns, "agg_ids": agg_ids}


def block_starts(agg_ids):
    count = agg_ids.shape[0]
    place = jnp.arange(count, dtype=jnp.int32)
    fresh = jnp.concatenate([jnp.ones((1,), dtype=bool), agg_ids[1:] != agg_ids[:-1]])
    return lax.cummax(jnp.where(fresh, place, 0).astype(jnp.int32), axis=0)


def reference(a_blocks, p_blocks, columns, agg_ids):
    count = p_blocks.shape[0]
    first = block_starts(agg_ids)
    pmat = p_blocks.reshape(count, BS, BS)
    lot = BLK_DEV

    def step(total, start):
        index = start + jnp.arange(lot, dtype=jnp.int32)
        amat = lax.dynamic_slice_in_dim(a_blocks, start, lot, 0).reshape(lot, NNZB, BS, BS).astype(jnp.float32)
        cols = lax.dynamic_slice_in_dim(columns, start, lot, 0)
        picked = pmat[cols].astype(jnp.float32)
        prods = jnp.einsum("ikpq,ikqr->ikpr", amat, picked)
        offs = agg_ids[cols] - agg_ids[index][:, None] + REACH
        select = (offs[..., None] == jnp.arange(BAND, dtype=jnp.int32)).astype(jnp.float32)
        band_rows = jnp.einsum("iko,ikpr->iopr", select, prods).astype(jnp.bfloat16)
        own = pmat[index].astype(jnp.float32)
        terms = jnp.einsum("iqp,ioqr->iopr", own, band_rows.astype(jnp.float32))
        total = total.at[first[index]].add(terms)
        return total, None

    starts = jnp.arange(count // lot, dtype=jnp.int32) * lot
    total = jnp.zeros((count, BAND, BS, BS), jnp.float32)
    total, unused = lax.scan(step, total, starts)
    return total.reshape(count, BAND, BS * BS).astype(jnp.bfloat16)
```

```python
import functools

import jax
import jax.numpy as jnp
from jax import lax
from jax.experimental import pallas as pl
from jax.experimental.pallas import tpu as pltpu
from jax.sharding import PartitionSpec as P

MESH = pl.DeviceIdType.MESH
BS = 64
NNZB = 6
REACH = 3
BAND = 7
ROWS = 16
NB = 4096
Q = 32
F32 = jnp.float32
BF16 = jnp.bfloat16


def dot(x, y):
    return lax.dot_general(x, y, (((1,), (0,)), ((), ())), preferred_element_type=F32)


def dot_nt(x, y):
    return lax.dot_general(x, y, (((1,), (1,)), ((), ())), preferred_element_type=F32)


def iota(shape, dim):
    return lax.broadcasted_iota(jnp.int32, shape, dim)


def segment(ids, g):
    last = NB - 1
    own = ids[g]
    start = jnp.logical_or(g == 0, ids[jnp.maximum(g - 1, 0)] != own)
    length = jnp.int32(1)
    for step in range(1, 4):
        same = jnp.logical_and(g + step <= last, ids[jnp.minimum(g + step, last)] == own)
        length = length + same.astype(jnp.int32)
    low = ids[jnp.maximum(g - REACH, 0)] - own + REACH
    high = ids[jnp.minimum(g + length - 1 + REACH, last)] - own + REACH
    return start, low, high, length


def kernel(K, ids, cols, a_ref, p_ref, out_ref, pscr, p2, hl, hr, dmat, lmat, ascr, blk, lead_out, lead_in, wire, wf, pk, sel, tab, ssem, rsem):
    t = lax.axis_index("tile")
    a = lax.axis_index("agg")
    rank = t * 4 + a
    base = rank * ROWS
    ranks = NB // ROWS
    nxt = lax.rem(rank + 1, ranks)
    prv = lax.rem(rank + ranks - 1, ranks)
    dev = lambda r: (r // 4, lax.rem(r, 4))
    sib = (t, a + 1 - 2 * lax.rem(a, 2))
    par = (t, lax.rem(a + 2, 4))
    bar = pltpu.get_barrier_semaphore()
    for d in (dev(nxt), dev(prv), sib, par):
        pl.semaphore_signal(bar, inc=1, device_id=d, device_id_type=MESH)

    pf = p_ref[...].astype(F32)
    for q in range(Q):
        pscr[pl.ds(q * ROWS, ROWS), :] = pf[:, q * 128:(q + 1) * 128]
    for i in range(ROWS):
        p2[pl.ds(i * Q, Q), :] = pscr[pl.ds(i, Q, stride=ROWS), :].astype(BF16)
    pl.semaphore_wait(bar, 4)

    def copy(src, dst, n, to):
        return pltpu.make_async_remote_copy(src_ref=src, dst_ref=dst, send_sem=ssem.at[n], recv_sem=rsem.at[n], device_id=to, device_id_type=MESH)

    H = REACH * Q
    c_right = copy(p2.at[pl.ds((ROWS - REACH) * Q, H)], hl, 0, dev(nxt))
    c_left = copy(p2.at[pl.ds(0, H)], hr, 1, dev(prv))
    c_right.start()
    c_left.start()

    r_, c_ = iota((128, 64), 0), iota((128, 64), 1)
    cc = lax.rem(r_, 64)
    flip = (lax.rem(cc, 2) != r_ // 64).astype(jnp.int32)
    spread = (c_ == cc // 2 + 32 * flip).astype(F32).astype(BF16)
    r2, l2 = iota((128, 128), 0), iota((128, 128), 1)
    diag = (r2 // 64) == (l2 // 64)
    low = iota((Q, 128), 1) < 64

    def spread_block(blockf):
        both = jnp.concatenate([blockf, pltpu.roll(blockf, 64, 1)], axis=0).astype(BF16)
        return jnp.where(diag, dot(spread, both), 0.0).astype(BF16)

    pr, pc = iota((64, 128), 0), iota((64, 128), 1)
    order = jnp.where(pr < 32, 2 * pr, 2 * (pr - 32) + 1)
    perm = (lax.rem(pc, 64) == order).astype(F32).astype(BF16)
    for i in range(ROWS):
        bf = p2[pl.ds(i * Q, Q), :].astype(F32)
        dmat[i + REACH] = spread_block(bf)
        split = jnp.concatenate([jnp.where(low, bf, 0.0), jnp.where(low, 0.0, bf)], axis=0).astype(BF16)
        lmat[pl.ds(i * 64, 64), :] = dot_nt(perm, split).astype(BF16)

    c_right.wait()
    c_left.wait()
    for i in range(REACH):
        dmat[i] = spread_block(hl[pl.ds(i * Q, Q), :].astype(F32))
        dmat[i + REACH + ROWS] = spread_block(hr[pl.ds(i * Q, Q), :].astype(F32))

    for k in range(NNZB):
        x = a_ref[k].astype(F32)
        for q in range(Q):
            ascr[pl.ds(k * 512 + q * ROWS, ROWS), :] = x[:, q * 128:(q + 1) * 128]

    acc = None
    for i in range(ROWS):
        own = ids[base + i]
        bands = [jnp.zeros((Q, 128), F32)] * 8
        for k in range(NNZB):
            a2 = ascr[pl.ds(k * 512 + i, Q, stride=ROWS), :].astype(BF16)
            j = cols[k, i]
            prod = dot(a2, dmat[jnp.clip(j - base + REACH, 0, ROWS + 2 * REACH - 1)])
            o = ids[j] - own + REACH
            for b in range(BAND):
                bands[b] = bands[b] + jnp.where(o == b, 1.0, 0.0).astype(F32) * prod
        ev, od = [], []
        for m in range(4):
            x0, x1 = bands[2 * m], bands[2 * m + 1]
            ev.append(jnp.where(low, x0, pltpu.roll(x1, 64, 1)))
            od.append(jnp.where(low, pltpu.roll(x0, 64, 1), x1))
        bcat = jnp.concatenate([jnp.concatenate(ev, axis=1), jnp.concatenate(od, axis=1)], axis=0).astype(BF16)
        term = dot(lmat[pl.ds(i * 64, 64), :], bcat)
        if acc is None:
            acc = term
        else:
            keep = jnp.where(ids[base + i - 1] == own, 1.0, 0.0).astype(F32)
            acc = term + keep * acc
        for m in range(4):
            x0, y0 = acc[:Q, m * 128:(m + 1) * 128], acc[Q:, m * 128:(m + 1) * 128]
            blk[i * 8 + 2 * m] = jnp.where(low, x0, pltpu.roll(y0, 64, 1))
            if m < 3:
                blk[i * 8 + 2 * m + 1] = jnp.where(low, pltpu.roll(x0, 64, 1), y0)
            else:
                blk[i * 8 + 7] = jnp.zeros((Q, 128), F32)
    blk[ROWS * 8] = jnp.zeros((Q, 128), F32)

    leads = jnp.where(jnp.logical_and(base > 0, ids[jnp.maximum(base - 1, 0)] == ids[base]), 1.0, 0.0).astype(F32)
    e = jnp.int32(0)
    run = jnp.int32(1)
    for step in range(1, 3):
        run = run * (ids[base + step] == ids[base]).astype(jnp.int32)
        e = e + run
    for o in range(BAND):
        lead_out[pl.ds(o * Q, Q), :] = (leads * blk[e * 8 + o]).astype(BF16)
    c_lead = copy(lead_out, lead_in, 2, dev(prv))
    c_lead.start()

    after = jnp.int32(ROWS)
    tab[0, ROWS], tab[1, ROWS], tab[2, ROWS], tab[3, ROWS] = jnp.int32(0), jnp.int32(1 << 20), jnp.int32(ROWS), jnp.int32(ROWS)
    for i in range(ROWS - 1, -1, -1):
        start, lo, hi, length = segment(ids, base + i)
        tab[0, i] = lo
        tab[1, i] = hi
        tab[2, i] = jnp.minimum(i + length - 1, ROWS - 1)
        tab[3, i] = after
        after = jnp.where(start, i, after)

    c_lead.wait()
    for o in range(BAND):
        at = (ROWS - 1) * 8 + o
        blk[at] = blk[at] + lead_in[pl.ds(o * Q, Q), :].astype(F32)

    s, o = after, tab[0, after]
    for m in range(K):
        at = jnp.minimum(tab[2, s] * 8 + o, ROWS * 8)
        wf[pl.ds(m, Q, stride=K), :] = blk[at]
        more = o < tab[1, s]
        s2 = jnp.where(more, s, tab[3, s])
        o = jnp.where(more, o + 1, tab[0, s2])
        s = s2
    wire[...] = wf[...].astype(BF16)

    c_sib = copy(wire, pk.at[0], 3, sib)
    c_par = copy(wire, pk.at[1], 4, par)
    c_par.start()
    c_sib.start()

    sources = [a, sib[1], par[1], lax.rem(sib[1] + 2, 4)]
    sub, lane = iota((ROWS, 128), 0), iota((ROWS, 128), 1)
    for d in range(4):
        count = jnp.int32(0)
        first = (t * 4 + sources[d]) * ROWS
        shift = jnp.zeros((ROWS, 128), jnp.int32)
        lows, highs = shift, shift
        for i in range(ROWS):
            start, lo, hi, length = segment(ids, first + i)
            here = sub == i
            lows = jnp.where(here, jnp.where(start, lo, 8), lows)
            highs = jnp.where(here, hi, highs)
            shift = jnp.where(here, count - lo, shift)
            count = count + jnp.where(start, hi - lo + 1, 0)
        for o in range(BAND):
            hit = jnp.logical_and(lane == shift + o, jnp.logical_and(lows <= o, highs >= o))
            sel[d, pl.ds(o * ROWS, ROWS), :] = jnp.where(hit, 1.0, 0.0).astype(BF16)

    def unpack(d, ref):
        at = pl.ds(pl.multiple_of(sources[d] * ROWS, ROWS), ROWS)
        hot = sel[d][:, :K]
        for q in range(0, Q, 2):
            w = jnp.concatenate([ref[pl.ds(q * K, K), :], ref[pl.ds((q + 1) * K, K), :]], axis=1)
            rows = dot(hot, w).astype(BF16)
            for o in range(BAND):
                out_ref[o, at, pl.ds(q * 128, 256)] = rows[o * ROWS:(o + 1) * ROWS]

    unpack(0, wire)
    c_sib.wait()
    unpack(1, pk.at[0])
    c_par.wait()
    c_fwd = copy(pk.at[1], pk.at[2], 5, sib)
    c_fwd.start()
    unpack(2, pk.at[1])
    c_fwd.wait()
    unpack(3, pk.at[2])


def run(K, cid, a_blocks, p_blocks, columns, agg_ids):
    vm = pltpu.VMEM
    out = pl.pallas_call(
        functools.partial(kernel, K),
        out_shape=jax.ShapeDtypeStruct((BAND, 4 * ROWS, BS * BS), BF16),
        in_specs=[pl.BlockSpec(memory_space=pltpu.SMEM)] * 2 + [pl.BlockSpec(memory_space=pltpu.VMEM)] * 2,
        out_specs=pl.BlockSpec(memory_space=pltpu.VMEM),
        scratch_shapes=[
            vm((Q * ROWS, 128), F32),
            vm((ROWS * Q, 128), BF16),
            vm((REACH * Q, 128), BF16),
            vm((REACH * Q, 128), BF16),
            vm((ROWS + 2 * REACH, 128, 128), BF16),
            vm((ROWS * 64, 64), BF16),
            vm((NNZB * Q * ROWS, 128), F32),
            vm((ROWS * 8 + 1, Q, 128), F32),
            vm((BAND * Q, 128), BF16),
            vm((BAND * Q, 128), BF16),
            vm((Q * K, 128), BF16),
            vm((Q * K, 128), F32),
            vm((3, Q * K, 128), BF16),
            vm((4, BAND * ROWS, 128), BF16),
            pltpu.SMEM((4, 32), jnp.int32),
            pltpu.SemaphoreType.DMA((6,)),
            pltpu.SemaphoreType.DMA((6,)),
        ],
        compiler_params=pltpu.CompilerParams(collective_id=cid, has_side_effects=True, vmem_limit_bytes=48 << 20),
    )(agg_ids, columns.T, jnp.transpose(a_blocks, (1, 0, 2)), p_blocks)
    return jnp.transpose(out, (1, 0, 2))


SLOTS = (48, 64, 112)


def most_blocks(ids):
    wide = jnp.pad(ids, (REACH, 2 * REACH), mode="edge")
    at = lambda step: lax.slice_in_dim(wide, REACH + step, REACH + step + NB)
    place = jnp.arange(NB, dtype=jnp.int32)
    start = jnp.logical_or(place == 0, at(-1) != ids)
    high = at(6)
    for length in (3, 2, 1):
        ends = jnp.logical_or(at(length) != ids, place + length >= NB)
        high = jnp.where(ends, at(length - 1 + REACH), high)
    count = jnp.where(start, high - at(-REACH) + 1, 0)
    return jnp.max(jnp.sum(count.reshape(NB // ROWS, ROWS), axis=1))


def local(a_blocks, p_blocks, columns, agg_ids):
    most = most_blocks(agg_ids)
    which = sum((most > k).astype(jnp.int32) for k in SLOTS[:-1])
    branches = [functools.partial(run, k, n) for n, k in enumerate(SLOTS)]
    return lax.switch(which, branches, a_blocks, p_blocks, columns, agg_ids)


def solution(mesh):
    return jax.shard_map(
        local,
        mesh=mesh,
        in_specs=(
            P(("tile", "agg"), None, None),
            P(("tile", "agg"), None),
            P(("tile", "agg"), None),
            P(),
        ),
        out_specs=P("tile", None, None),
        check_vma=False,
    )
```

```python
import functools

import jax
import jax.numpy as jnp
from jax import lax
from jax.experimental import pallas as pl
from jax.experimental.pallas import tpu as pltpu
from jax.sharding import PartitionSpec as P

MESH = pl.DeviceIdType.MESH
BS = 64
NNZB = 6
REACH = 3
BAND = 7
ROWS = 16
NB = 4096
Q = 32
CHUNK = 8
EARLY = 16
LAST_EARLY = 12
CLASSES = ((24, 48, 4), (32, 48, 4), (96, 96, 1))
F32 = jnp.float32
BF16 = jnp.bfloat16
I32 = jnp.int32


def dot(x, y):
    return lax.dot_general(x, y, (((1,), (0,)), ((), ())), preferred_element_type=F32)


def dot_nt(x, y):
    return lax.dot_general(x, y, (((1,), (1,)), ((), ())), preferred_element_type=F32)


def iota(shape, dim):
    return lax.broadcasted_iota(I32, shape, dim)


def choose(ids_ref, out_ref):
    ids = ids_ref[...]
    row, lane = iota((Q, 128), 0), iota((Q, 128), 1)
    flat = row * 128 + lane
    final = jnp.max(ids)

    def at(step):
        moved = pltpu.roll(ids, (-step) % 128, 1)
        other = pltpu.roll(moved, (Q - 1) if step > 0 else 1, 0)
        inside = lane + step < 128 if step > 0 else lane + step >= 0
        got = jnp.where(inside, moved, other)
        return jnp.where(flat + step >= NB, final, jnp.where(flat + step < 0, 0, got))

    start = jnp.logical_or(flat == 0, at(-1) != ids)
    high = at(6)
    length = jnp.full((Q, 128), 4, I32)
    for n in (3, 2, 1):
        ends = jnp.logical_or(at(n) != ids, flat + n >= NB)
        high = jnp.where(ends, at(n - 1 + REACH), high)
        length = jnp.where(ends, n, length)
    count = jnp.where(start, high - at(-REACH) + 1, 0)
    early = jnp.where(lax.rem(lane, ROWS) + length - 1 <= LAST_EARLY, count, 0)
    sums = (iota((128, 128), 0) // ROWS == iota((128, 128), 1)).astype(F32).astype(BF16)
    total = dot(count.astype(F32).astype(BF16), sums)
    rest = total - jnp.minimum(dot(early.astype(F32).astype(BF16), sums), float(EARLY))
    pair = jnp.where(lax.rem(lane, 2) == 0, rest + pltpu.roll(rest, 127, 1), 0.0)
    most_pair, most = jnp.max(pair).astype(I32), jnp.max(rest).astype(I32)
    which = jnp.int32(0)
    for slots, own, _ in CLASSES[:-1]:
        which = which + jnp.logical_or(most_pair > 2 * slots, most > own).astype(I32)
    out_ref[0] = which


def segment(ids, g):
    last = NB - 1
    own = ids[g]
    start = jnp.logical_or(g == 0, ids[jnp.maximum(g - 1, 0)] != own)
    length = jnp.int32(1)
    for step in range(1, 4):
        same = jnp.logical_and(g + step <= last, ids[jnp.minimum(g + step, last)] == own)
        length = length + same.astype(I32)
    low = ids[jnp.maximum(g - REACH, 0)] - own + REACH
    high = ids[jnp.minimum(g + length - 1 + REACH, last)] - own + REACH
    return start, low, high, length


def kernel(KB, KL, PH, ids, cols, a_ref, p_ref, out_ref, pscr, p2, hl, hr, dmat, lmat, ascr, blk, lead_out, lead_in,
           wa, wb, own_l, own_rows, sib_a, sib_l, sib_rows, pka, pkb, wf, sel_own, sel_a, sel_b, tab, walk, ssem, rsem):
    t = lax.axis_index("tile")
    a = lax.axis_index("agg")
    rank = t * 4 + a
    base = rank * ROWS
    ranks = NB // ROWS
    nxt = lax.rem(rank + 1, ranks)
    prv = lax.rem(rank + ranks - 1, ranks)
    dev = lambda r: (r // 4, lax.rem(r, 4))
    sib_at = a + 1 - 2 * lax.rem(a, 2)
    par_at = lax.rem(a + 2, 4)
    dia_at = lax.rem(sib_at + 2, 4)
    sib, par = (t, sib_at), (t, par_at)
    bar = pltpu.get_barrier_semaphore()
    for d in (dev(nxt), dev(prv), sib, par):
        pl.semaphore_signal(bar, inc=1, device_id=d, device_id_type=MESH)

    def copy(src, dst, n, to):
        return pltpu.make_async_remote_copy(src_ref=src, dst_ref=dst, send_sem=ssem.at[n], recv_sem=rsem.at[n], device_id=to, device_id_type=MESH)

    pf = p_ref[...].astype(F32)
    for q in range(Q):
        pscr[pl.ds(q * ROWS, ROWS), :] = pf[:, q * 128:(q + 1) * 128]
    for i in range(ROWS):
        p2[pl.ds(i * Q, Q), :] = pscr[pl.ds(i, Q, stride=ROWS), :].astype(BF16)
    pl.semaphore_wait(bar, 4)
    H = REACH * Q
    c_right = copy(p2.at[pl.ds((ROWS - REACH) * Q, H)], hl, 0, dev(nxt))
    c_left = copy(p2.at[pl.ds(0, H)], hr, 1, dev(prv))
    c_right.start()
    c_left.start()

    after, mine, mine_early = jnp.int32(ROWS), jnp.int32(0), jnp.int32(0)
    tab[0, ROWS], tab[1, ROWS], tab[2, ROWS], tab[3, ROWS] = jnp.int32(0), jnp.int32(1 << 20), jnp.int32(ROWS), jnp.int32(ROWS)
    for i in range(ROWS - 1, -1, -1):
        start, lo, hi, length = segment(ids, base + i)
        tab[0, i] = lo
        tab[1, i] = hi
        tab[2, i] = jnp.minimum(i + length - 1, ROWS - 1)
        tab[3, i] = after
        after = jnp.where(start, i, after)
        here = jnp.where(start, hi - lo + 1, 0)
        mine = mine + here
        mine_early = mine_early + jnp.where(i + length - 1 <= LAST_EARLY, here, 0)
    mine_rest = mine - jnp.minimum(mine_early, EARLY)
    s, o = after, tab[0, after]
    for m in range(EARLY + KL):
        end = tab[2, s]
        fits = end <= LAST_EARLY if m < EARLY else end >= 0
        walk[m] = jnp.where(fits, jnp.clip(end * 8 + o, 0, ROWS * 8), ROWS * 8)
        more = jnp.logical_or(o < tab[1, s], jnp.logical_not(fits))
        s2 = jnp.where(more, s, tab[3, s])
        o = jnp.where(more, o + fits.astype(I32), tab[0, s2])
        s = s2

    r_, c_ = iota((128, 64), 0), iota((128, 64), 1)
    cc = lax.rem(r_, 64)
    flip = (lax.rem(cc, 2) != r_ // 64).astype(I32)
    spread = (c_ == cc // 2 + 32 * flip).astype(F32).astype(BF16)
    diag = (iota((128, 128), 0) // 64) == (iota((128, 128), 1) // 64)
    low = iota((Q, 128), 1) < 64

    def spread_block(blockf):
        both = jnp.concatenate([blockf, pltpu.roll(blockf, 64, 1)], axis=0).astype(BF16)
        return jnp.where(diag, dot(spread, both), 0.0).astype(BF16)

    pr, pc = iota((64, 128), 0), iota((64, 128), 1)
    order = jnp.where(pr < 32, 2 * pr, 2 * (pr - 32) + 1)
    perm = (lax.rem(pc, 64) == order).astype(F32).astype(BF16)
    for i in range(ROWS):
        bf = p2[pl.ds(i * Q, Q), :].astype(F32)
        dmat[i + REACH] = spread_block(bf)
        split = jnp.concatenate([jnp.where(low, bf, 0.0), jnp.where(low, 0.0, bf)], axis=0).astype(BF16)
        lmat[pl.ds(i * 64, 64), :] = dot_nt(perm, split).astype(BF16)
    for k in range(NNZB):
        x = a_ref[k].astype(F32)
        for q in range(Q):
            ascr[pl.ds(k * 512 + q * ROWS, ROWS), :] = x[:, q * 128:(q + 1) * 128]

    def row(i, acc):
        own = ids[base + i]
        bands = [jnp.zeros((Q, 128), F32)] * 8
        for k in range(NNZB):
            a2 = ascr[pl.ds(k * 512 + i, Q, stride=ROWS), :].astype(BF16)
            j = cols[k, i]
            prod = dot(a2, dmat[jnp.clip(j - base + REACH, 0, ROWS + 2 * REACH - 1)])
            o = ids[j] - own + REACH
            for b in range(BAND):
                bands[b] = bands[b] + jnp.where(o == b, 1.0, 0.0).astype(F32) * prod
        ev, od = [], []
        for m in range(4):
            x0, x1 = bands[2 * m], bands[2 * m + 1]
            ev.append(jnp.where(low, x0, pltpu.roll(x1, 64, 1)))
            od.append(jnp.where(low, pltpu.roll(x0, 64, 1), x1))
        bcat = jnp.concatenate([jnp.concatenate(ev, axis=1), jnp.concatenate(od, axis=1)], axis=0).astype(BF16)
        term = dot(lmat[pl.ds(i * 64, 64), :], bcat)
        if acc is not None:
            term = term + jnp.where(ids[base + i - 1] == own, 1.0, 0.0).astype(F32) * acc
        for m in range(4):
            x0, y0 = term[:Q, m * 128:(m + 1) * 128], term[Q:, m * 128:(m + 1) * 128]
            blk[i * 8 + 2 * m] = jnp.where(low, x0, pltpu.roll(y0, 64, 1))
            if m < 3:
                blk[i * 8 + 2 * m + 1] = jnp.where(low, pltpu.roll(x0, 64, 1), y0)
        return term

    acc = None
    for i in range(REACH, ROWS - REACH):
        acc = row(i, acc)
    blk[ROWS * 8] = jnp.zeros((Q, 128), F32)
    c_right.wait()
    c_left.wait()
    for i in range(REACH):
        dmat[i] = spread_block(hl[pl.ds(i * Q, Q), :].astype(F32))
        dmat[i + REACH + ROWS] = spread_block(hr[pl.ds(i * Q, Q), :].astype(F32))
    first = None
    for i in range(REACH):
        first = row(i, first)

    leads = jnp.where(jnp.logical_and(base > 0, ids[jnp.maximum(base - 1, 0)] == ids[base]), 1.0, 0.0).astype(F32)
    e, run = jnp.int32(0), jnp.int32(1)
    for step in range(1, REACH):
        run = run * (ids[base + step] == ids[base]).astype(I32)
        e = e + run
    for o in range(BAND):
        lead_out[pl.ds(o * Q, Q), :] = (leads * blk[e * 8 + o]).astype(BF16)
    c_lead = copy(lead_out, lead_in, 2, dev(prv))
    c_lead.start()
    for i in range(REACH, 2 * REACH):
        joined = jnp.where(ids[base + i] == ids[base + REACH - 1], 1.0, 0.0).astype(F32)
        for o in range(BAND):
            blk[i * 8 + o] = blk[i * 8 + o] + joined * blk[(REACH - 1) * 8 + o]

    for m in range(EARLY):
        wf[pl.ds(m, Q, stride=EARLY), :] = blk[walk[m]]
    wa[...] = wf[pl.ds(0, Q * EARLY), :].astype(BF16)
    c_a_par = copy(wa, pka.at[0], 3, par)
    c_a_sib = copy(wa, sib_a, 4, sib)
    c_a_par.start()
    c_a_sib.start()

    for i in range(ROWS - REACH, ROWS):
        acc = row(i, acc)
    c_lead.wait()
    for o in range(BAND):
        at = (ROWS - 1) * 8 + o
        blk[at] = blk[at] + lead_in[pl.ds(o * Q, Q), :].astype(F32)
    for m in range(KL):
        own_l[pl.ds(m * Q, Q), :] = blk[walk[EARLY + m]].astype(BF16)
    c_l_sib = copy(own_l, sib_l, 5, sib)
    c_l_sib.start()
    c_l_sib.wait()
    for h in range(KB):
        v = own_l[pl.ds(h * Q, Q), :].astype(F32)
        m = 2 * KB - 1 - h
        if m < KL:
            v = jnp.where(h < mine_rest, v, sib_l[pl.ds(m * Q, Q), :].astype(F32))
        wf[pl.ds(h, Q, stride=KB), :] = v
    part = CHUNK * KB
    c_b = []
    for g in range(Q // CHUNK):
        at = pl.ds(g * part, part)
        wb[at, :] = wf[at, :].astype(BF16)
        c_b.append(copy(wb.at[at], pkb.at[0, at], 7 + g, par))
        c_b[-1].start()

    sub, lane = iota((ROWS, 128), 0), iota((ROWS, 128), 1)

    def places(which):
        count, early = jnp.int32(0), jnp.int32(0)
        begin = (t * 4 + which) * ROWS
        shift = jnp.zeros((ROWS, 128), I32)
        lows, highs, ends = shift, shift, shift
        for i in range(ROWS):
            start, lo, hi, length = segment(ids, begin + i)
            here = sub == i
            lows = jnp.where(here, jnp.where(start, lo, 8), lows)
            highs = jnp.where(here, hi, highs)
            shift = jnp.where(here, count - lo, shift)
            ends = jnp.where(here, i + length - 1, ends)
            more = jnp.where(start, hi - lo + 1, 0)
            count = count + more
            early = early + jnp.where(i + length - 1 <= LAST_EARLY, more, 0)
        early = jnp.minimum(early, EARLY)
        out = []
        for o in range(BAND):
            n = shift + o
            there = jnp.logical_and(lows <= o, highs >= o)
            is_early = jnp.logical_and(ends <= LAST_EARLY, n < EARLY)
            out.append((there, is_early, n, n - early))
        return out

    def hot(cond):
        return jnp.where(cond, 1.0, 0.0).astype(BF16)

    for u, which in enumerate((a, sib_at)):
        for o, (there, is_early, n, m) in enumerate(places(which)):
            col = jnp.where(is_early, n + u * EARLY, m + 2 * EARLY + u * KL)
            col = jnp.where(there, col, -1)
            for c in range(sel_own.shape[1] // 128):
                sel_own[pl.ds((o * 2 + u) * ROWS, ROWS), pl.ds(c * 128, 128)] = hot(col == lane + c * 128)
    for u, which in enumerate((par_at, dia_at)):
        for o, (there, is_early, n, m) in enumerate(places(which)):
            col_a = jnp.where(jnp.logical_and(there, is_early), n + u * PH * EARLY, -(1 << 20))
            col_b = jnp.where(m < KB, m + u * PH * KB, 2 * KB - 1 - m + (1 - u) * PH * KB)
            col_b = jnp.where(jnp.logical_and(there, jnp.logical_not(is_early)), col_b, -(1 << 20))
            for p in range(PH):
                at = pl.ds(((p * BAND + o) * 2 + u) * ROWS, ROWS)
                sel_a[at, :] = hot(col_a + p * EARLY == lane)
                for c in range(sel_b.shape[1] // 128):
                    sel_b[at, pl.ds(c * 128, 128)] = hot(col_b + p * KB == lane + c * 128)

    def put(rows, q, where):
        for o in range(BAND):
            for u in range(2):
                at = pl.ds(pl.multiple_of(where[u] * ROWS, ROWS), ROWS)
                out_ref[o, at, pl.ds(q * 128, 128)] = rows[(o * 2 + u) * ROWS:(o * 2 + u + 1) * ROWS]

    c_a_sib.wait()
    for m in range(KL):
        wf[pl.ds(m, Q, stride=KL), :] = own_l[pl.ds(m * Q, Q), :].astype(F32)
    own_rows[...] = wf[pl.ds(0, Q * KL), :].astype(BF16)
    for m in range(KL):
        wf[pl.ds(m, Q, stride=KL), :] = sib_l[pl.ds(m * Q, Q), :].astype(F32)
    sib_rows[...] = wf[pl.ds(0, Q * KL), :].astype(BF16)
    for q in range(0, Q, 2):
        two = []
        for x in (q, q + 1):
            ea, el = pl.ds(x * EARLY, EARLY), pl.ds(x * KL, KL)
            two.append(jnp.concatenate([wa[ea, :], sib_a[ea, :], own_rows[el, :], sib_rows[el, :]], axis=0))
        got = dot(sel_own[:, :2 * (EARLY + KL)], jnp.concatenate(two, axis=1)).astype(BF16)
        put(got[:, :128], q, (a, sib_at))
        put(got[:, 128:], q + 1, (a, sib_at))

    c_a_par.wait()
    c_a_fwd = copy(pka.at[0], pka.at[1], 6, sib)
    c_a_fwd.start()
    c_f = []
    for g in range(Q // CHUNK):
        at = pl.ds(g * part, part)
        c_b[g].wait()
        c_f.append(copy(pkb.at[0, at], pkb.at[1, at], 11 + g, sib))
        c_f[-1].start()
        if g == 0:
            c_a_fwd.wait()
        if g > 0:
            c_f[g - 1].wait()
            unpack_far(g - 1, PH, KB, pka, pkb, sel_a, sel_b, put, (par_at, dia_at))
    g = Q // CHUNK - 1
    c_f[g].wait()
    unpack_far(g, PH, KB, pka, pkb, sel_a, sel_b, put, (par_at, dia_at))


def unpack_far(g, PH, KB, pka, pkb, sel_a, sel_b, put, where):
    for f in range(CHUNK // (2 * PH)):
        q = g * CHUNK + f * 2 * PH
        wide_a, wide_b = [], []
        for x in (q, q + PH):
            wide_a.append(jnp.concatenate([pka[u, pl.ds(x * EARLY, PH * EARLY), :] for u in range(2)], axis=0))
            wide_b.append(jnp.concatenate([pkb[u, pl.ds(x * KB, PH * KB), :] for u in range(2)], axis=0))
        rows_a = dot(sel_a[:, :2 * PH * EARLY], jnp.concatenate(wide_a, axis=1))
        rows_b = dot(sel_b[:, :2 * PH * KB], jnp.concatenate(wide_b, axis=1))
        got = (rows_a + rows_b).astype(BF16)
        for p in range(PH):
            rows = got[p * BAND * 2 * ROWS:(p + 1) * BAND * 2 * ROWS]
            put(rows[:, :128], q + p, where)
            put(rows[:, 128:], q + PH + p, where)


def run(n, a_blocks, p_blocks, columns, agg_ids):
    KB, KL, PH = CLASSES[n]
    vm = pltpu.VMEM
    up = lambda x: -(-x // 128) * 128
    out = pl.pallas_call(
        functools.partial(kernel, KB, KL, PH),
        out_shape=jax.ShapeDtypeStruct((BAND, 4 * ROWS, BS * BS), BF16),
        in_specs=[pl.BlockSpec(memory_space=pltpu.SMEM)] * 2 + [pl.BlockSpec(memory_space=pltpu.VMEM)] * 2,
        out_specs=pl.BlockSpec(memory_space=pltpu.VMEM),
        scratch_shapes=[
            vm((Q * ROWS, 128), F32),
            vm((ROWS * Q, 128), BF16),
            vm((REACH * Q, 128), BF16),
            vm((REACH * Q, 128), BF16),
            vm((ROWS + 2 * REACH, 128, 128), BF16),
            vm((ROWS * 64, 64), BF16),
            vm((NNZB * Q * ROWS, 128), F32),
            vm((ROWS * 8 + 1, Q, 128), F32),
            vm((BAND * Q, 128), BF16),
            vm((BAND * Q, 128), BF16),
            vm((Q * EARLY, 128), BF16),
            vm((Q * KB, 128), BF16),
            vm((Q * KL, 128), BF16),
            vm((Q * KL, 128), BF16),
            vm((Q * EARLY, 128), BF16),
            vm((Q * KL, 128), BF16),
            vm((Q * KL, 128), BF16),
            vm((2, Q * EARLY, 128), BF16),
            vm((2, Q * KB, 128), BF16),
            vm((Q * max(KL, KB), 128), F32),
            vm((2 * BAND * ROWS, up(2 * (EARLY + KL))), BF16),
            vm((PH * 2 * BAND * ROWS, 128), BF16),
            vm((PH * 2 * BAND * ROWS, up(2 * PH * KB)), BF16),
            pltpu.SMEM((4, 32), I32),
            pltpu.SMEM((EARLY + KL,), I32),
            pltpu.SemaphoreType.DMA((15,)),
            pltpu.SemaphoreType.DMA((15,)),
        ],
        compiler_params=pltpu.CompilerParams(collective_id=n, has_side_effects=True, vmem_limit_bytes=48 << 20),
    )(agg_ids, columns.T, jnp.transpose(a_blocks, (1, 0, 2)), p_blocks)
    return jnp.transpose(out, (1, 0, 2))


def local(a_blocks, p_blocks, columns, agg_ids):
    which = pl.pallas_call(
        choose,
        out_shape=jax.ShapeDtypeStruct((1,), I32),
        in_specs=[pl.BlockSpec(memory_space=pltpu.VMEM)],
        out_specs=pl.BlockSpec(memory_space=pltpu.SMEM),
    )(agg_ids.reshape(Q, 128))
    branches = [functools.partial(run, n) for n in range(len(CLASSES))]
    return lax.switch(which[0], branches, a_blocks, p_blocks, columns, agg_ids)


def solution(mesh):
    return jax.shard_map(
        local,
        mesh=mesh,
        in_specs=(
            P(("tile", "agg"), None, None),
            P(("tile", "agg"), None),
            P(("tile", "agg"), None),
            P(),
        ),
        out_specs=P("tile", None, None),
        check_vma=False,
    )
```

```python
import functools

import jax
import jax.numpy as jnp
from jax import lax
from jax.experimental import pallas as pl
from jax.experimental.pallas import tpu as pltpu
from jax.sharding import PartitionSpec as P

MESH = pl.DeviceIdType.MESH
BS = 64
NNZB = 6
REACH = 3
BAND = 7
ROWS = 16
NB = 4096
Q = 32
CHUNK = 8
PARTS = ((8, 1), (8, 2), (8, 3))
EARLY = sum(f for f, _ in PARTS)
LAST = 9
NEAR = 2
CLASSES = ((16, 2), (24, 2), (112, 2))
F32 = jnp.float32
BF16 = jnp.bfloat16
I32 = jnp.int32


def dot(x, y):
    return lax.dot_general(x, y, (((1,), (0,)), ((), ())), preferred_element_type=F32)


def dot_nt(x, y):
    return lax.dot_general(x, y, (((1,), (1,)), ((), ())), preferred_element_type=F32)


def iota(shape, dim):
    return lax.broadcasted_iota(I32, shape, dim)


def level(place, length):
    end = place + length - 1
    soon = jnp.logical_and(place >= REACH, end <= LAST)
    return jnp.where(soon, 1, jnp.where(end < ROWS - REACH, 2, 3))


def choose(ids_ref, out_ref):
    ids = ids_ref[...]
    row, lane = iota((Q, 128), 0), iota((Q, 128), 1)
    flat = row * 128 + lane
    final = jnp.max(ids)

    def at(step):
        moved = pltpu.roll(ids, (-step) % 128, 1)
        other = pltpu.roll(moved, (Q - 1) if step > 0 else 1, 0)
        inside = lane + step < 128 if step > 0 else lane + step >= 0
        got = jnp.where(inside, moved, other)
        return jnp.where(flat + step >= NB, final, jnp.where(flat + step < 0, 0, got))

    start = jnp.logical_or(flat == 0, at(-1) != ids)
    high = at(6)
    length = jnp.full((Q, 128), 4, I32)
    for n in (3, 2, 1):
        ends = jnp.logical_or(at(n) != ids, flat + n >= NB)
        high = jnp.where(ends, at(n - 1 + REACH), high)
        length = jnp.where(ends, n, length)
    count = jnp.where(start, high - at(-REACH) + 1, 0)
    place = lax.rem(lane, ROWS)
    grade = level(place, length)
    sums = (iota((128, 128), 0) // ROWS == iota((128, 128), 1)).astype(F32).astype(BF16)
    upto = [jnp.where(grade <= most, count, 0).astype(F32).astype(BF16) for _, most in PARTS]
    upto = dot(jnp.concatenate(upto + [count.astype(F32).astype(BF16)], axis=0), sums)
    used = 0.0
    for n, (slots, _) in enumerate(PARTS):
        used = used + jnp.minimum(upto[n * Q:(n + 1) * Q] - used, float(slots))
    rest = upto[len(PARTS) * Q:] - used
    pair = jnp.where(lax.rem(lane, 2) == 0, rest + pltpu.roll(rest, 127, 1), 0.0)
    most = jnp.max(pair)
    which = jnp.int32(0)
    for slots, _ in CLASSES[:-1]:
        which = which + (most > float(2 * slots)).astype(I32)
    out_ref[0] = which


def segment(ids, g):
    last = NB - 1
    own = ids[g]
    start = jnp.logical_or(g == 0, ids[jnp.maximum(g - 1, 0)] != own)
    length = jnp.int32(1)
    for step in range(1, 4):
        same = jnp.logical_and(g + step <= last, ids[jnp.minimum(g + step, last)] == own)
        length = length + same.astype(I32)
    low = ids[jnp.maximum(g - REACH, 0)] - own + REACH
    high = ids[jnp.minimum(g + length - 1 + REACH, last)] - own + REACH
    return start, low, high, length


def parts_of(upto):
    ends, used = [], 0
    for n, (slots, _) in enumerate(PARTS):
        used = used + jnp.minimum(upto[n] - used, slots)
        ends.append(used)
    return ends


def kernel(KB, PH, ids_in, cols_in, a_in, p_in, out_ref, ids, cols, a_ref, p_ref, pscr, p2, hl, hr, dmat, lmat, ascr, blk, lead_out, lead_in, lead_rows, lead_mine,
           wa, sib_a, pka, wb, pkb, own_l, own_rows, sib_l, sib_rows, wf, sel_near, sel_far, tab, walk, lsem, ssem, rsem):
    KL = 2 * KB
    t = lax.axis_index("tile")
    a = lax.axis_index("agg")
    rank = t * 4 + a
    base = rank * ROWS
    ranks = NB // ROWS
    nxt = lax.rem(rank + 1, ranks)
    prv = lax.rem(rank + ranks - 1, ranks)
    dev = lambda r: (r // 4, lax.rem(r, 4))
    sib_at = a + 1 - 2 * lax.rem(a, 2)
    par_at = lax.rem(a + 2, 4)
    dia_at = lax.rem(sib_at + 2, 4)
    sib, par = (t, sib_at), (t, par_at)
    bar = pltpu.get_barrier_semaphore()
    for d in (dev(nxt), dev(prv), sib, par):
        pl.semaphore_signal(bar, inc=1, device_id=d, device_id_type=MESH)
    tiles = ranks // 4
    before = lax.rem(t + tiles - 1, tiles)

    @pl.when(a == 0)
    def _():
        for d in (lax.rem(t + 1, tiles), before):
            pl.semaphore_signal(bar, inc=1, device_id=(d, a), device_id_type=MESH)


    def copy(src, dst, n, to):
        return pltpu.make_async_remote_copy(src_ref=src, dst_ref=dst, send_sem=ssem.at[n], recv_sem=rsem.at[n], device_id=to, device_id_type=MESH)

    loads = [pltpu.make_async_copy(x, y, lsem.at[n]) for n, (x, y) in enumerate(((p_in, p_ref), (ids_in, ids), (cols_in, cols), (a_in, a_ref)))]
    for c in loads:
        c.start()
    loads[0].wait()

    pf = p_ref[...].astype(F32)
    for q in range(Q):
        pscr[pl.ds(q * ROWS, ROWS), :] = pf[:, q * 128:(q + 1) * 128]
    for i in range(ROWS):
        p2[pl.ds(i * Q, Q), :] = pscr[pl.ds(i, Q, stride=ROWS), :].astype(BF16)
    pl.semaphore_wait(bar, 4 + 2 * (a == 0).astype(I32))
    H = REACH * Q
    c_right = copy(p2.at[pl.ds((ROWS - REACH) * Q, H)], hl, 0, dev(nxt))
    c_left = copy(p2.at[pl.ds(0, H)], hr, 1, dev(prv))
    c_right.start()
    c_left.start()

    loads[1].wait()

    tab[0, ROWS], tab[1, ROWS], tab[2, ROWS], tab[3, ROWS], tab[4, ROWS] = jnp.int32(0), jnp.int32(1 << 20), jnp.int32(ROWS), jnp.int32(ROWS), jnp.int32(9)
    starts, grades = [], []
    upto = [jnp.int32(0)] * (len(PARTS) + 1)
    for i in range(ROWS):
        start, lo, hi, length = segment(ids, base + i)
        grade = level(i, length)
        starts.append(start)
        grades.append(grade)
        tab[0, i] = lo
        tab[1, i] = hi
        tab[2, i] = jnp.minimum(i + length - 1, ROWS - 1)
        tab[4, i] = grade
        here = jnp.where(start, hi - lo + 1, 0)
        for n in range(len(PARTS) + 1):
            upto[n] = upto[n] + (jnp.where(grade <= PARTS[n][1], here, 0) if n < len(PARTS) else here)
    after = jnp.int32(ROWS)
    link = [None] * ROWS
    for i in range(ROWS - 1, REACH - 1, -1):
        link[i] = after
        after = jnp.where(jnp.logical_and(starts[i], grades[i] > 1), i, after)
    for i in range(REACH - 1, -1, -1):
        link[i] = after
        after = jnp.where(starts[i], i, after)
    for i in range(ROWS - 1, REACH - 1, -1):
        soon = jnp.logical_and(starts[i], grades[i] == 1)
        link[i] = jnp.where(soon, after, link[i])
        after = jnp.where(soon, i, after)
    for i in range(ROWS):
        tab[3, i] = link[i]
    mine_rest = upto[-1] - parts_of(upto)[-1]
    s, o = after, tab[0, after]
    m = 0
    for slots, most in PARTS + ((KL, 99),):
        for _ in range(slots):
            end = tab[2, s]
            fits = tab[4, s] <= most
            walk[m] = jnp.where(fits, jnp.clip(end * 8 + o, 0, ROWS * 8), ROWS * 8)
            more = jnp.logical_or(o < tab[1, s], jnp.logical_not(fits))
            s2 = jnp.where(more, s, tab[3, s])
            o = jnp.where(more, o + fits.astype(I32), tab[0, s2])
            s = s2
            m += 1

    r_, c_ = iota((128, 64), 0), iota((128, 64), 1)
    cc = lax.rem(r_, 64)
    flip = (lax.rem(cc, 2) != r_ // 64).astype(I32)
    spread = (c_ == cc // 2 + 32 * flip).astype(F32).astype(BF16)
    diag = (iota((128, 128), 0) // 64) == (iota((128, 128), 1) // 64)
    low = iota((Q, 128), 1) < 64

    def spread_block(blockf):
        both = jnp.concatenate([blockf, pltpu.roll(blockf, 64, 1)], axis=0).astype(BF16)
        return jnp.where(diag, dot(spread, both), 0.0).astype(BF16)

    pr, pc = iota((64, 128), 0), iota((64, 128), 1)
    order = jnp.where(pr < 32, 2 * pr, 2 * (pr - 32) + 1)
    perm = (lax.rem(pc, 64) == order).astype(F32).astype(BF16)
    for i in range(ROWS):
        bf = p2[pl.ds(i * Q, Q), :].astype(F32)
        dmat[i + REACH] = spread_block(bf)
        split = jnp.concatenate([jnp.where(low, bf, 0.0), jnp.where(low, 0.0, bf)], axis=0).astype(BF16)
        lmat[pl.ds(i * 64, 64), :] = dot_nt(perm, split).astype(BF16)
    loads[2].wait()
    loads[3].wait()
    for k in range(NNZB):
        x = a_ref[k].astype(F32)
        for q in range(Q):
            ascr[pl.ds(k * 512 + q * ROWS, ROWS), :] = x[:, q * 128:(q + 1) * 128]

    def row(i, acc):
        own = ids[base + i]
        bands = [jnp.zeros((Q, 128), F32)] * 8
        for k in range(NNZB):
            a2 = ascr[pl.ds(k * 512 + i, Q, stride=ROWS), :].astype(BF16)
            j = cols[k, i]
            prod = dot(a2, dmat[jnp.clip(j - base + REACH, 0, ROWS + 2 * REACH - 1)])
            o = ids[j] - own + REACH
            for b in range(BAND):
                bands[b] = bands[b] + jnp.where(o == b, 1.0, 0.0).astype(F32) * prod
        ev, od = [], []
        for m in range(4):
            x0, x1 = bands[2 * m], bands[2 * m + 1]
            ev.append(jnp.where(low, x0, pltpu.roll(x1, 64, 1)))
            od.append(jnp.where(low, pltpu.roll(x0, 64, 1), x1))
        bcat = jnp.concatenate([jnp.concatenate(ev, axis=1), jnp.concatenate(od, axis=1)], axis=0).astype(BF16)
        term = dot(lmat[pl.ds(i * 64, 64), :], bcat)
        if acc is not None:
            term = term + jnp.where(ids[base + i - 1] == own, 1.0, 0.0).astype(F32) * acc
        for m in range(4):
            x0, y0 = term[:Q, m * 128:(m + 1) * 128], term[Q:, m * 128:(m + 1) * 128]
            blk[i * 8 + 2 * m] = jnp.where(low, x0, pltpu.roll(y0, 64, 1))
            if m < 3:
                blk[i * 8 + 2 * m + 1] = jnp.where(low, pltpu.roll(x0, 64, 1), y0)
        return term

    def early(n):
        first = sum(f for f, _ in PARTS[:n])
        slots = PARTS[n][0]
        for m in range(slots):
            wf[pl.ds(m, Q, stride=slots), :] = blk[walk[first + m]]
        wa[n] = wf[pl.ds(0, Q * slots), :].astype(BF16)
        to_par, to_sib = copy(wa.at[n], pka.at[0, n], 6 + 2 * n, par), copy(wa.at[n], sib_a.at[n], 7 + 2 * n, sib)
        to_par.start()
        to_sib.start()
        return to_par, to_sib

    blk[ROWS * 8] = jnp.zeros((Q, 128), F32)
    acc = None
    c_early = []
    for i in range(REACH, ROWS - REACH):
        acc = row(i, acc)
        if i == LAST:
            c_early.append(early(0))
    c_right.wait()
    c_left.wait()
    for i in range(REACH):
        dmat[i] = spread_block(hl[pl.ds(i * Q, Q), :].astype(F32))
        dmat[i + REACH + ROWS] = spread_block(hr[pl.ds(i * Q, Q), :].astype(F32))
    first = None
    for i in range(REACH):
        first = row(i, first)

    leads = jnp.where(jnp.logical_and(base > 0, ids[jnp.maximum(base - 1, 0)] == ids[base]), 1.0, 0.0).astype(F32)
    e, run = jnp.int32(0), jnp.int32(1)
    for step in range(1, REACH):
        run = run * (ids[base + step] == ids[base]).astype(I32)
        e = e + run
    odd = lax.rem(a, 2) == 1
    inner = jnp.where(odd, leads, 0.0)
    for o in range(BAND):
        v = blk[e * 8 + o]
        lead_out[pl.ds(o * Q, Q), :] = (inner * v).astype(BF16)
        wf[pl.ds(o, Q, stride=8), :] = leads * v
    wf[pl.ds(BAND, Q, stride=8), :] = jnp.zeros((Q, 128), F32)
    lead_mine[...] = wf[pl.ds(0, Q * 8), :].astype(BF16)
    c_lead = copy(lead_out, lead_in, 2, sib)
    c_lead.start()

    def outer(k):
        to = t if k == 0 else before
        return [pltpu.make_async_remote_copy(src_ref=lead_mine, dst_ref=lead_rows.at[k], send_sem=ssem.at[23 + n], recv_sem=rsem.at[23 + k], device_id=(to, d), device_id_type=MESH) for n, d in enumerate((0, 3))]

    for k in range(2):
        @pl.when(a == 2 - 2 * k)
        def _(k=k):
            for c in outer(k):
                c.start()

    for i in range(REACH, 2 * REACH):
        joined = jnp.where(ids[base + i] == ids[base + REACH - 1], 1.0, 0.0).astype(F32)
        for o in range(BAND):
            blk[i * 8 + o] = blk[i * 8 + o] + joined * blk[(REACH - 1) * 8 + o]

    c_early.append(early(1))
    for i in range(ROWS - REACH, ROWS):
        acc = row(i, acc)
    c_lead.wait()
    for o in range(BAND):
        at = (ROWS - 1) * 8 + o
        blk[at] = blk[at] + lead_in[pl.ds(o * Q, Q), :].astype(F32)
    c_early.append(early(2))
    for m in range(KB, KL):
        own_l[pl.ds(m * Q, Q), :] = blk[walk[EARLY + m]].astype(BF16)
    tail, body = pl.ds(KB * Q, KB * Q), pl.ds(0, KB * Q)
    c_tail = copy(own_l.at[tail], sib_l.at[tail], 3, sib)
    c_tail.start()
    for m in range(KB):
        own_l[pl.ds(m * Q, Q), :] = blk[walk[EARLY + m]].astype(BF16)
    c_body = copy(own_l.at[body], sib_l.at[body], 4, sib)
    c_body.start()
    c_tail.wait()
    for h in range(KB):
        v = own_l[pl.ds(h * Q, Q), :].astype(F32)
        v = jnp.where(h < mine_rest, v, sib_l[pl.ds((KL - 1 - h) * Q, Q), :].astype(F32))
        wf[pl.ds(h, Q, stride=KB), :] = v
    part = CHUNK * KB
    c_b = []
    for g in range(Q // CHUNK):
        at = pl.ds(g * part, part)
        wb[at, :] = wf[at, :].astype(BF16)
        c_b.append(copy(wb.at[at], pkb.at[0, at], 15 + g, par))
        c_b[-1].start()

    sub, lane = iota((ROWS, 128), 0), iota((ROWS, 128), 1)

    def places(which):
        begin = (t * 4 + which) * ROWS
        zero = jnp.zeros((ROWS, 128), I32)
        shift, lows, highs = zero, zero + 8, zero
        found = [segment(ids, begin + i) for i in range(ROWS)]
        grades = [level(i, found[i][3]) for i in range(ROWS)]
        here = [jnp.where(start, hi - lo + 1, 0) for start, lo, hi, _ in found]
        upto = [sum(jnp.where(grades[i] <= most, here[i], 0) for i in range(ROWS)) for _, most in PARTS] + [sum(here)]
        soon, later = jnp.int32(0), upto[0]
        for i in range(ROWS):
            start, lo, hi, _ = found[i]
            row_i = sub == i
            lows = jnp.where(row_i, jnp.where(start, lo, 8), lows)
            highs = jnp.where(row_i, hi, highs)
            shift = jnp.where(row_i, jnp.where(grades[i] == 1, soon, later) - lo, shift)
            soon = soon + jnp.where(grades[i] == 1, here[i], 0)
            later = later + jnp.where(grades[i] == 1, 0, here[i])
        ends = parts_of(upto)
        final = jnp.int32(0)
        for i in range(ROWS):
            final = jnp.where(found[i][0], i, final)
        final = jnp.where(lax.rem(which, 2) == 1, final, -1)
        return [(jnp.logical_and(lows <= o, highs >= o), shift + o) for o in range(BAND)], ends, final

    def build(sel, P_, pair, last, shared):
        for u, which in enumerate(pair):
            blocks, ends, final = places(which)
            for o, (there, n) in enumerate(blocks):
                m = n - ends[-1]
                if shared:
                    col = jnp.where(m < last, m + u * P_ * last, 2 * last - 1 - m + (1 - u) * P_ * last)
                else:
                    col = m + u * P_ * last
                col = col + 2 * P_ * EARLY
                step = jnp.full((ROWS, 128), last, I32)
                for k in range(len(PARTS) - 1, -1, -1):
                    slots = PARTS[k][0]
                    inside = n < ends[k]
                    begin = ends[k - 1] if k else 0
                    base_col = 2 * P_ * sum(f for f, _ in PARTS[:k]) + u * P_ * slots
                    col = jnp.where(inside, n - begin + base_col, col)
                    step = jnp.where(inside, slots, step)
                col = jnp.where(there, col, -(1 << 20))
                col2 = jnp.where(sub == final, 2 * P_ * (EARLY + last) + o, -(1 << 20))
                for p in range(P_):
                    at = pl.ds(((p * BAND + o) * 2 + u) * ROWS, ROWS)
                    for c in range(sel.shape[1] // 128):
                        sel[at, pl.ds(c * 128, 128)] = jnp.where(jnp.logical_or(col == lane + c * 128, col2 == lane + c * 128), 1.0, 0.0).astype(BF16)
                    col, col2 = col + step, col2 + 8

    def unpack(q, P_, sel, early_of, rest_of, last, where, lead):
        wide = []
        for x in (q, q + P_):
            tall = []
            for n, (slots, _) in enumerate(PARTS):
                tall += [early_of(u, n, pl.ds(x * slots, P_ * slots)) for u in range(2)]
            tall += [rest_of(u, pl.ds(x * last, P_ * last)) for u in range(2)]
            tall.append(lead_rows[lead, pl.ds(x * 8, P_ * 8), :])
            wide.append(jnp.concatenate(tall, axis=0))
        got = dot(sel[:, :2 * P_ * (EARLY + last) + 8 * P_], jnp.concatenate(wide, axis=1)).astype(BF16)
        for p in range(P_):
            for o in range(BAND):
                for u in range(2):
                    at = pl.ds(pl.multiple_of(where[u] * ROWS, ROWS), ROWS)
                    rows = got[((p * BAND + o) * 2 + u) * ROWS:((p * BAND + o) * 2 + u + 1) * ROWS]
                    out_ref[o, at, pl.ds((q + p) * 128, 128)] = rows[:, :128]
                    out_ref[o, at, pl.ds((q + P_ + p) * 128, 128)] = rows[:, 128:]

    build(sel_near, NEAR, (a, sib_at), KL, False)
    for m in range(KL):
        wf[pl.ds(m, Q, stride=KL), :] = own_l[pl.ds(m * Q, Q), :].astype(F32)
    own_rows[...] = wf[pl.ds(0, Q * KL), :].astype(BF16)
    for _, to_sib in c_early:
        to_sib.wait()
    c_body.wait()
    for m in range(KL):
        wf[pl.ds(m, Q, stride=KL), :] = sib_l[pl.ds(m * Q, Q), :].astype(F32)
    sib_rows[...] = wf[pl.ds(0, Q * KL), :].astype(BF16)
    near_early = lambda u, n, at: (wa, sib_a)[u][n, at, :]
    near_rest = lambda u, at: (own_rows, sib_rows)[u][at, :]
    c_on = []
    for n, (to_par, _) in enumerate(c_early):
        to_par.wait()
        c_on.append(copy(pka.at[0, n], pka.at[1, n], 12 + n, sib))
        c_on[-1].start()
    first_hop = [pltpu.make_async_remote_copy(src_ref=lead_mine, dst_ref=lead_rows.at[k], send_sem=ssem.at[23], recv_sem=rsem.at[23 + k], device_id=sib, device_id_type=MESH) for k in range(2)]
    second_hop = [copy(lead_rows.at[k], lead_rows.at[k], 25 + k, sib) for k in range(2)]
    ends_here = jnp.logical_or(a == 0, a == 3)

    @pl.when(ends_here)
    def _():
        for k in range(2):
            first_hop[k].wait_recv()
            second_hop[k].start()
        for k in range(2):
            second_hop[k].wait_send()

    @pl.when(jnp.logical_not(ends_here))
    def _():
        for k in range(2):
            second_hop[k].wait_recv()

    for k in range(2):
        @pl.when(a == 2 - 2 * k)
        def _(k=k):
            for c in outer(k):
                c.wait_send()

    for q in range(0, Q, 2 * NEAR):
        unpack(q, NEAR, sel_near, near_early, near_rest, KL, (a, sib_at), a // 2)

    build(sel_far, PH, (par_at, dia_at), KB, True)
    far_early = lambda u, n, at: pka[u, n, at, :]
    far_rest = lambda u, at: pkb[u, at, :]
    for c in c_on:
        c.wait()
    c_f = []
    for g in range(Q // CHUNK + 1):
        if g < Q // CHUNK:
            at = pl.ds(g * part, part)
            c_b[g].wait()
            c_f.append(copy(pkb.at[0, at], pkb.at[1, at], 19 + g, sib))
            c_f[g].start()
        if g > 0:
            c_f[g - 1].wait()
            for q in range((g - 1) * CHUNK, g * CHUNK, 2 * PH):
                unpack(q, PH, sel_far, far_early, far_rest, KB, (par_at, dia_at), 1 - a // 2)


def run(n, a_blocks, p_blocks, columns, agg_ids):
    KB, PH = CLASSES[n]
    KL = 2 * KB
    vm = pltpu.VMEM
    up = lambda x: -(-x // 128) * 128
    out = pl.pallas_call(
        functools.partial(kernel, KB, PH),
        out_shape=jax.ShapeDtypeStruct((BAND, 4 * ROWS, BS * BS), BF16),
        in_specs=[pl.BlockSpec(memory_space=pl.ANY)] * 4,
        out_specs=pl.BlockSpec(memory_space=pltpu.VMEM),
        scratch_shapes=[
            pltpu.SMEM((NB,), I32),
            pltpu.SMEM((NNZB, ROWS), I32),
            vm((NNZB, ROWS, BS * BS), BF16),
            vm((ROWS, BS * BS), BF16),
            vm((Q * ROWS, 128), F32),
            vm((ROWS * Q, 128), BF16),
            vm((REACH * Q, 128), BF16),
            vm((REACH * Q, 128), BF16),
            vm((ROWS + 2 * REACH, 128, 128), BF16),
            vm((ROWS * 64, 64), BF16),
            vm((NNZB * Q * ROWS, 128), F32),
            vm((ROWS * 8 + 1, Q, 128), F32),
            vm((BAND * Q, 128), BF16),
            vm((BAND * Q, 128), BF16),
            vm((2, Q * 8, 128), BF16),
            vm((Q * 8, 128), BF16),
            vm((len(PARTS), Q * PARTS[0][0], 128), BF16),
            vm((len(PARTS), Q * PARTS[0][0], 128), BF16),
            vm((2, len(PARTS), Q * PARTS[0][0], 128), BF16),
            vm((Q * KB, 128), BF16),
            vm((2, Q * KB, 128), BF16),
            vm((Q * KL, 128), BF16),
            vm((Q * KL, 128), BF16),
            vm((Q * KL, 128), BF16),
            vm((Q * KL, 128), BF16),
            vm((Q * KL, 128), F32),
            vm((NEAR * 2 * BAND * ROWS, up(2 * NEAR * (EARLY + KL) + 8 * NEAR)), BF16),
            vm((PH * 2 * BAND * ROWS, up(2 * PH * (EARLY + KB) + 8 * PH)), BF16),
            pltpu.SMEM((8, 32), I32),
            pltpu.SMEM((EARLY + KL,), I32),
            pltpu.SemaphoreType.DMA((4,)),
            pltpu.SemaphoreType.DMA((27,)),
            pltpu.SemaphoreType.DMA((27,)),
        ],
        compiler_params=pltpu.CompilerParams(collective_id=n, has_side_effects=True, vmem_limit_bytes=48 << 20),
    )(agg_ids, columns.T, jnp.transpose(a_blocks, (1, 0, 2)), p_blocks)
    return jnp.transpose(out, (1, 0, 2))


def local(a_blocks, p_blocks, columns, agg_ids):
    which = pl.pallas_call(
        choose,
        out_shape=jax.ShapeDtypeStruct((1,), I32),
        in_specs=[pl.BlockSpec(memory_space=pltpu.VMEM)],
        out_specs=pl.BlockSpec(memory_space=pltpu.SMEM),
    )(agg_ids.reshape(Q, 128))
    branches = [functools.partial(run, n) for n in range(len(CLASSES))]
    return lax.switch(which[0], branches, a_blocks, p_blocks, columns, agg_ids)


def solution(mesh):
    return jax.shard_map(
        local,
        mesh=mesh,
        in_specs=(
            P(("tile", "agg"), None, None),
            P(("tile", "agg"), None),
            P(("tile", "agg"), None),
            P(),
        ),
        out_specs=P("tile", None, None),
        check_vma=False,
    )
```

```python
import functools

import jax
import jax.numpy as jnp
from jax import lax
from jax.experimental import pallas as pl
from jax.experimental.pallas import tpu as pltpu
from jax.sharding import PartitionSpec as P

MESH = pl.DeviceIdType.MESH
BS = 64
NNZB = 6
REACH = 3
BAND = 7
ROWS = 16
NB = 4096
Q = 32
CHUNK = 8
PARTS = ((8, 1), (8, 2), (8, 3))
EARLY = sum(f for f, _ in PARTS)
LAST = 9
NEAR = 2
CLASSES = ((16, 2), (24, 2), (112, 2))
F32 = jnp.float32
BF16 = jnp.bfloat16
I32 = jnp.int32


def dot(x, y):
    return lax.dot_general(x, y, (((1,), (0,)), ((), ())), preferred_element_type=F32)


def dot_nt(x, y):
    return lax.dot_general(x, y, (((1,), (1,)), ((), ())), preferred_element_type=F32)


def iota(shape, dim):
    return lax.broadcasted_iota(I32, shape, dim)


def level(place, length):
    end = place + length - 1
    soon = jnp.logical_and(place >= REACH, end <= LAST)
    return jnp.where(soon, 1, jnp.where(end < ROWS - REACH, 2, 3))


def choose(ids_ref, out_ref):
    ids = ids_ref[...]
    row, lane = iota((Q, 128), 0), iota((Q, 128), 1)
    flat = row * 128 + lane
    final = jnp.max(ids)

    def at(step):
        moved = pltpu.roll(ids, (-step) % 128, 1)
        other = pltpu.roll(moved, (Q - 1) if step > 0 else 1, 0)
        inside = lane + step < 128 if step > 0 else lane + step >= 0
        got = jnp.where(inside, moved, other)
        return jnp.where(flat + step >= NB, final, jnp.where(flat + step < 0, 0, got))

    start = jnp.logical_or(flat == 0, at(-1) != ids)
    high = at(6)
    length = jnp.full((Q, 128), 4, I32)
    for n in (3, 2, 1):
        ends = jnp.logical_or(at(n) != ids, flat + n >= NB)
        high = jnp.where(ends, at(n - 1 + REACH), high)
        length = jnp.where(ends, n, length)
    count = jnp.where(start, high - at(-REACH) + 1, 0)
    place = lax.rem(lane, ROWS)
    grade = level(place, length)
    sums = (iota((128, 128), 0) // ROWS == iota((128, 128), 1)).astype(F32).astype(BF16)
    upto = [jnp.where(grade <= most, count, 0).astype(F32).astype(BF16) for _, most in PARTS]
    upto = dot(jnp.concatenate(upto + [count.astype(F32).astype(BF16)], axis=0), sums)
    used = 0.0
    for n, (slots, _) in enumerate(PARTS):
        used = used + jnp.minimum(upto[n * Q:(n + 1) * Q] - used, float(slots))
    rest = upto[len(PARTS) * Q:] - used
    pair = jnp.where(lax.rem(lane, 2) == 0, rest + pltpu.roll(rest, 127, 1), 0.0)
    most = jnp.max(pair)
    which = jnp.int32(0)
    for slots, _ in CLASSES[:-1]:
        which = which + (most > float(2 * slots)).astype(I32)
    out_ref[0] = which


def segment(ids, g):
    last = NB - 1
    own = ids[g]
    start = jnp.logical_or(g == 0, ids[jnp.maximum(g - 1, 0)] != own)
    length = jnp.int32(1)
    for step in range(1, 4):
        same = jnp.logical_and(g + step <= last, ids[jnp.minimum(g + step, last)] == own)
        length = length + same.astype(I32)
    low = ids[jnp.maximum(g - REACH, 0)] - own + REACH
    high = ids[jnp.minimum(g + length - 1 + REACH, last)] - own + REACH
    return start, low, high, length


def parts_of(upto):
    ends, used = [], 0
    for n, (slots, _) in enumerate(PARTS):
        used = used + jnp.minimum(upto[n] - used, slots)
        ends.append(used)
    return ends


def each(begin, end, body):
    if end - begin <= 64:
        for m in range(begin, end):
            body(m)
    else:
        pl.loop(begin, end)(body)


def kernel(KB, PH, ids_in, cols_in, a_in, p_in, out_ref, ids, cols, a_ref, p_ref, pscr, p2, hl, hr, dmat, lmat, ascr, bscr, blk, lead_out, lead_in, lead_far, lead_rows,
           wa, sib_a, pka, wb, pkb, own_l, own_rows, sib_l, sib_rows, wf, sel_near, sel_far, tab, walk, lsem, ssem, rsem):
    KL = 2 * KB
    t = lax.axis_index("tile")
    a = lax.axis_index("agg")
    rank = t * 4 + a
    base = rank * ROWS
    ranks = NB // ROWS
    nxt = lax.rem(rank + 1, ranks)
    prv = lax.rem(rank + ranks - 1, ranks)
    dev = lambda r: (r // 4, lax.rem(r, 4))
    sib_at = a + 1 - 2 * lax.rem(a, 2)
    par_at = lax.rem(a + 2, 4)
    dia_at = lax.rem(sib_at + 2, 4)
    sib, par = (t, sib_at), (t, par_at)
    bar = pltpu.get_barrier_semaphore()
    for d in (dev(nxt), dev(prv), sib, par):
        pl.semaphore_signal(bar, inc=1, device_id=d, device_id_type=MESH)
    tiles = ranks // 4
    before = lax.rem(t + tiles - 1, tiles)

    @pl.when(a == 0)
    def _():
        for d in (lax.rem(t + 1, tiles), before):
            pl.semaphore_signal(bar, inc=1, device_id=(d, a), device_id_type=MESH)


    def copy(src, dst, n, to):
        return pltpu.make_async_remote_copy(src_ref=src, dst_ref=dst, send_sem=ssem.at[n], recv_sem=rsem.at[n], device_id=to, device_id_type=MESH)

    loads = [pltpu.make_async_copy(x, y, lsem.at[n]) for n, (x, y) in enumerate(((p_in, p_ref), (ids_in, ids), (cols_in, cols), (a_in, a_ref)))]
    for c in loads:
        c.start()
    loads[0].wait()

    pf = p_ref[...].astype(F32)
    for q in range(Q):
        pscr[pl.ds(q * ROWS, ROWS), :] = pf[:, q * 128:(q + 1) * 128]
    for i in range(ROWS):
        p2[pl.ds(i * Q, Q), :] = pscr[pl.ds(i, Q, stride=ROWS), :].astype(BF16)
    H = REACH * Q
    c_right = copy(p2.at[pl.ds((ROWS - REACH) * Q, H)], hl, 0, dev(nxt))
    c_left = copy(p2.at[pl.ds(0, H)], hr, 1, dev(prv))

    def meet():
        pl.semaphore_wait(bar, 4 + 2 * (a == 0).astype(I32))
        c_right.start()
        c_left.start()

    @pl.when(a >= 2)
    def _():
        meet()


    loads[1].wait()

    tab[0, ROWS], tab[1, ROWS], tab[2, ROWS], tab[3, ROWS], tab[4, ROWS] = jnp.int32(0), jnp.int32(1 << 20), jnp.int32(ROWS), jnp.int32(ROWS), jnp.int32(9)
    starts, grades = [], []
    upto = [jnp.int32(0)] * (len(PARTS) + 1)
    for i in range(ROWS):
        start, lo, hi, length = segment(ids, base + i)
        grade = level(i, length)
        starts.append(start)
        grades.append(grade)
        tab[0, i] = lo
        tab[1, i] = hi
        tab[2, i] = jnp.minimum(i + length - 1, ROWS - 1)
        tab[4, i] = grade
        here = jnp.where(start, hi - lo + 1, 0)
        for n in range(len(PARTS) + 1):
            upto[n] = upto[n] + (jnp.where(grade <= PARTS[n][1], here, 0) if n < len(PARTS) else here)
    after = jnp.int32(ROWS)
    link = [None] * ROWS
    for i in range(ROWS - 1, REACH - 1, -1):
        link[i] = after
        after = jnp.where(jnp.logical_and(starts[i], grades[i] > 1), i, after)
    for i in range(REACH - 1, -1, -1):
        link[i] = after
        after = jnp.where(starts[i], i, after)
    for i in range(ROWS - 1, REACH - 1, -1):
        soon = jnp.logical_and(starts[i], grades[i] == 1)
        link[i] = jnp.where(soon, after, link[i])
        after = jnp.where(soon, i, after)
    for i in range(ROWS):
        tab[3, i] = link[i]
    mine_rest = upto[-1] - parts_of(upto)[-1]
    def step(most, m, state):
        s, o = state
        end = tab[2, s]
        fits = tab[4, s] <= most
        walk[m] = jnp.where(fits, jnp.clip(end * 8 + o, 0, ROWS * 8), ROWS * 8)
        more = jnp.logical_or(o < tab[1, s], jnp.logical_not(fits))
        s2 = jnp.where(more, s, tab[3, s])
        return s2, jnp.where(more, o + fits.astype(I32), tab[0, s2])

    state, m = (after, tab[0, after]), 0
    for slots, most in PARTS + ((KL, 99),):
        if slots <= 64:
            for _ in range(slots):
                state = step(most, m, state)
                m += 1
        else:
            state = lax.fori_loop(m, m + slots, functools.partial(step, most), state)

    r_, c_ = iota((128, 64), 0), iota((128, 64), 1)
    cc = lax.rem(r_, 64)
    flip = (lax.rem(cc, 2) != r_ // 64).astype(I32)
    spread = (c_ == cc // 2 + 32 * flip).astype(F32).astype(BF16)
    diag = (iota((128, 128), 0) // 64) == (iota((128, 128), 1) // 64)
    low = iota((Q, 128), 1) < 64

    def spread_block(blockf):
        both = jnp.concatenate([blockf, pltpu.roll(blockf, 64, 1)], axis=0).astype(BF16)
        return jnp.where(diag, dot(spread, both), 0.0).astype(BF16)

    pr, pc = iota((64, 128), 0), iota((64, 128), 1)
    order = jnp.where(pr < 32, 2 * pr, 2 * (pr - 32) + 1)
    perm = (lax.rem(pc, 64) == order).astype(F32).astype(BF16)
    for i in range(ROWS):
        bf = p2[pl.ds(i * Q, Q), :].astype(F32)
        dmat[i + REACH] = spread_block(bf)
        split = jnp.concatenate([jnp.where(low, bf, 0.0), jnp.where(low, 0.0, bf)], axis=0).astype(BF16)
        lmat[pl.ds(i * 64, 64), :] = dot_nt(perm, split).astype(BF16)
    loads[2].wait()
    loads[3].wait()
    for k in range(NNZB):
        x = a_ref[k].astype(F32)
        for q in range(Q):
            ascr[pl.ds(k * 512 + q * ROWS, ROWS), :] = x[:, q * 128:(q + 1) * 128]

    def products(i):
        own = ids[base + i]
        bands = [jnp.zeros((Q, 128), F32)] * 8
        for k in range(NNZB):
            a2 = ascr[pl.ds(k * 512 + i, Q, stride=ROWS), :].astype(BF16)
            j = cols[k, i]
            prod = dot(a2, dmat[jnp.clip(j - base + REACH, 0, ROWS + 2 * REACH - 1)])
            o = ids[j] - own + REACH
            for b in range(BAND):
                bands[b] = bands[b] + jnp.where(o == b, 1.0, 0.0).astype(F32) * prod
        ev, od = [], []
        for m in range(4):
            x0, x1 = bands[2 * m], bands[2 * m + 1]
            ev.append(jnp.where(low, x0, pltpu.roll(x1, 64, 1)))
            od.append(jnp.where(low, pltpu.roll(x0, 64, 1), x1))
        bscr[i] = jnp.concatenate([jnp.concatenate(ev, axis=1), jnp.concatenate(od, axis=1)], axis=0).astype(BF16)

    def row(i, acc):
        term = dot(lmat[pl.ds(i * 64, 64), :], bscr[i])
        if acc is not None:
            term = term + jnp.where(ids[base + i - 1] == ids[base + i], 1.0, 0.0).astype(F32) * acc
        for m in range(4):
            x0, y0 = term[:Q, m * 128:(m + 1) * 128], term[Q:, m * 128:(m + 1) * 128]
            blk[i * 8 + 2 * m] = jnp.where(low, x0, pltpu.roll(y0, 64, 1))
            if m < 3:
                blk[i * 8 + 2 * m + 1] = jnp.where(low, pltpu.roll(x0, 64, 1), y0)
        return term

    def rows(begin, end, acc):
        for i in range(begin, end):
            products(i)
        for i in range(begin, end):
            acc = row(i, acc)
        return acc

    def early(n):
        first = sum(f for f, _ in PARTS[:n])
        slots = PARTS[n][0]
        for m in range(slots):
            wf[pl.ds(m, Q, stride=slots), :] = blk[walk[first + m]]
        wa[n] = wf[pl.ds(0, Q * slots), :].astype(BF16)
        to_par, to_sib = copy(wa.at[n], pka.at[0, n], 6 + 2 * n, par), copy(wa.at[n], sib_a.at[n], 7 + 2 * n, sib)
        to_par.start()
        to_sib.start()
        return to_par, to_sib

    blk[ROWS * 8] = jnp.zeros((Q, 128), F32)
    c_early = []
    acc = rows(REACH, LAST + 1, None)

    @pl.when(a < 2)
    def _():
        meet()

    c_early.append(early(0))
    acc = rows(LAST + 1, ROWS - REACH, acc)
    c_right.wait()
    c_left.wait()
    for i in range(REACH):
        dmat[i] = spread_block(hl[pl.ds(i * Q, Q), :].astype(F32))
        dmat[i + REACH + ROWS] = spread_block(hr[pl.ds(i * Q, Q), :].astype(F32))
    rows(0, REACH, None)

    leads = jnp.where(jnp.logical_and(base > 0, ids[jnp.maximum(base - 1, 0)] == ids[base]), 1.0, 0.0).astype(F32)
    e, run = jnp.int32(0), jnp.int32(1)
    for step in range(1, REACH):
        run = run * (ids[base + step] == ids[base]).astype(I32)
        e = e + run
    for o in range(BAND):
        lead_out[pl.ds(o * Q, Q), :] = (leads * blk[e * 8 + o]).astype(BF16)
    c_lead = copy(lead_out, lead_in, 2, sib)
    c_lead.start()

    def outer(k):
        to = t if k == 0 else before
        return [pltpu.make_async_remote_copy(src_ref=lead_out, dst_ref=lead_far.at[k], send_sem=ssem.at[23 + n], recv_sem=rsem.at[23 + k], device_id=(to, d), device_id_type=MESH) for n, d in enumerate((0, 3))]

    for k in range(2):
        @pl.when(a == 2 - 2 * k)
        def _(k=k):
            for c in outer(k):
                c.start()

    for i in range(REACH, 2 * REACH):
        joined = jnp.where(ids[base + i] == ids[base + REACH - 1], 1.0, 0.0).astype(F32)
        for o in range(BAND):
            blk[i * 8 + o] = blk[i * 8 + o] + joined * blk[(REACH - 1) * 8 + o]

    c_early.append(early(1))
    rows(ROWS - REACH, ROWS, acc)
    c_lead.wait()
    even = jnp.where(lax.rem(a, 2) == 0, 1.0, 0.0).astype(F32)
    for o in range(BAND):
        at = (ROWS - 1) * 8 + o
        blk[at] = blk[at] + even * lead_in[pl.ds(o * Q, Q), :].astype(F32)
    c_early.append(early(2))
    def keep(m):
        own_l[pl.ds(pl.multiple_of(m * Q, Q), Q), :] = blk[walk[EARLY + m]].astype(BF16)

    each(KB, KL, keep)
    tail, body = pl.ds(KB * Q, KB * Q), pl.ds(0, KB * Q)
    c_tail = copy(own_l.at[tail], sib_l.at[tail], 3, sib)
    c_tail.start()
    each(0, KB, keep)
    c_body = copy(own_l.at[body], sib_l.at[body], 4, sib)
    c_body.start()
    c_tail.wait()

    def share(h):
        v = own_l[pl.ds(pl.multiple_of(h * Q, Q), Q), :].astype(F32)
        v = jnp.where(h < mine_rest, v, sib_l[pl.ds(pl.multiple_of((KL - 1 - h) * Q, Q), Q), :].astype(F32))
        wf[pl.ds(h, Q, stride=KB), :] = v

    each(0, KB, share)
    part = CHUNK * KB
    c_b = []
    for g in range(Q // CHUNK):
        at = pl.ds(g * part, part)
        wb[at, :] = wf[at, :].astype(BF16)
        c_b.append(copy(wb.at[at], pkb.at[0, at], 15 + g, par))
        c_b[-1].start()

    sub, lane = iota((ROWS, 128), 0), iota((ROWS, 128), 1)

    def places(which):
        begin = (t * 4 + which) * ROWS
        zero = jnp.zeros((ROWS, 128), I32)
        shift, lows, highs = zero, zero + 8, zero
        found = [segment(ids, begin + i) for i in range(ROWS)]
        grades = [level(i, found[i][3]) for i in range(ROWS)]
        here = [jnp.where(start, hi - lo + 1, 0) for start, lo, hi, _ in found]
        upto = [sum(jnp.where(grades[i] <= most, here[i], 0) for i in range(ROWS)) for _, most in PARTS] + [sum(here)]
        soon, later = jnp.int32(0), upto[0]
        for i in range(ROWS):
            start, lo, hi, _ = found[i]
            row_i = sub == i
            lows = jnp.where(row_i, jnp.where(start, lo, 8), lows)
            highs = jnp.where(row_i, hi, highs)
            shift = jnp.where(row_i, jnp.where(grades[i] == 1, soon, later) - lo, shift)
            soon = soon + jnp.where(grades[i] == 1, here[i], 0)
            later = later + jnp.where(grades[i] == 1, 0, here[i])
        ends = parts_of(upto)
        final = jnp.int32(0)
        for i in range(ROWS):
            final = jnp.where(found[i][0], i, final)
        final = jnp.where(lax.rem(which, 2) == 1, final, -1)
        return [(jnp.logical_and(lows <= o, highs >= o), shift + o) for o in range(BAND)], ends, final

    def build(sel, P_, pair, last, shared):
        for u, which in enumerate(pair):
            blocks, ends, final = places(which)
            for o, (there, n) in enumerate(blocks):
                m = n - ends[-1]
                if shared:
                    col = jnp.where(m < last, m + u * P_ * last, 2 * last - 1 - m + (1 - u) * P_ * last)
                else:
                    col = m + u * P_ * last
                col = col + 2 * P_ * EARLY
                step = jnp.full((ROWS, 128), last, I32)
                for k in range(len(PARTS) - 1, -1, -1):
                    slots = PARTS[k][0]
                    inside = n < ends[k]
                    begin = ends[k - 1] if k else 0
                    base_col = 2 * P_ * sum(f for f, _ in PARTS[:k]) + u * P_ * slots
                    col = jnp.where(inside, n - begin + base_col, col)
                    step = jnp.where(inside, slots, step)
                col = jnp.where(there, col, -(1 << 20))
                col2 = jnp.where(sub == final, 2 * P_ * (EARLY + last) + o, -(1 << 20))
                for p in range(P_):
                    at = pl.ds(((p * BAND + o) * 2 + u) * ROWS, ROWS)
                    for c in range(sel.shape[1] // 128):
                        sel[at, pl.ds(c * 128, 128)] = jnp.where(jnp.logical_or(col == lane + c * 128, col2 == lane + c * 128), 1.0, 0.0).astype(BF16)
                    col, col2 = col + step, col2 + 8

    def unpack(q, P_, sel, early_of, rest_of, last, where, lead):
        wide = []
        for x in (q, q + P_):
            tall = []
            for n, (slots, _) in enumerate(PARTS):
                tall += [early_of(u, n, pl.ds(x * slots, P_ * slots)) for u in range(2)]
            tall += [rest_of(u, pl.ds(x * last, P_ * last)) for u in range(2)]
            tall.append(lead_rows[lead, pl.ds(x * 8, P_ * 8), :])
            wide.append(jnp.concatenate(tall, axis=0))
        got = dot(sel[:, :2 * P_ * (EARLY + last) + 8 * P_], jnp.concatenate(wide, axis=1)).astype(BF16)
        for p in range(P_):
            for o in range(BAND):
                for u in range(2):
                    at = pl.ds(pl.multiple_of(where[u] * ROWS, ROWS), ROWS)
                    rows = got[((p * BAND + o) * 2 + u) * ROWS:((p * BAND + o) * 2 + u + 1) * ROWS]
                    out_ref[o, at, pl.ds((q + p) * 128, 128)] = rows[:, :128]
                    out_ref[o, at, pl.ds((q + P_ + p) * 128, 128)] = rows[:, 128:]

    build(sel_near, NEAR, (a, sib_at), KL, False)
    def lay(ref, m):
        wf[pl.ds(m, Q, stride=KL), :] = ref[pl.ds(pl.multiple_of(m * Q, Q), Q), :].astype(F32)

    each(0, KL, functools.partial(lay, own_l))
    own_rows[...] = wf[pl.ds(0, Q * KL), :].astype(BF16)
    for _, to_sib in c_early:
        to_sib.wait()
    c_body.wait()
    each(0, KL, functools.partial(lay, sib_l))
    sib_rows[...] = wf[pl.ds(0, Q * KL), :].astype(BF16)
    near_early = lambda u, n, at: (wa, sib_a)[u][n, at, :]
    near_rest = lambda u, at: (own_rows, sib_rows)[u][at, :]
    c_on = []
    for n, (to_par, _) in enumerate(c_early):
        to_par.wait()
        c_on.append(copy(pka.at[0, n], pka.at[1, n], 12 + n, sib))
        c_on[-1].start()
    first_hop = [pltpu.make_async_remote_copy(src_ref=lead_out, dst_ref=lead_far.at[k], send_sem=ssem.at[23], recv_sem=rsem.at[23 + k], device_id=sib, device_id_type=MESH) for k in range(2)]
    second_hop = [copy(lead_far.at[k], lead_far.at[k], 25 + k, sib) for k in range(2)]
    ends_here = jnp.logical_or(a == 0, a == 3)

    @pl.when(ends_here)
    def _():
        for k in range(2):
            first_hop[k].wait_recv()
            second_hop[k].start()
        for k in range(2):
            second_hop[k].wait_send()

    @pl.when(jnp.logical_not(ends_here))
    def _():
        for k in range(2):
            second_hop[k].wait_recv()

    for k in range(2):
        @pl.when(a == 2 - 2 * k)
        def _(k=k):
            for c in outer(k):
                c.wait_send()

    for k in range(2):
        for o in range(BAND):
            wf[pl.ds(o, Q, stride=8), :] = lead_far[k, pl.ds(o * Q, Q), :].astype(F32)
        wf[pl.ds(BAND, Q, stride=8), :] = jnp.zeros((Q, 128), F32)
        lead_rows[k] = wf[pl.ds(0, Q * 8), :].astype(BF16)
    for q in range(0, Q, 2 * NEAR):
        unpack(q, NEAR, sel_near, near_early, near_rest, KL, (a, sib_at), a // 2)

    build(sel_far, PH, (par_at, dia_at), KB, True)
    far_early = lambda u, n, at: pka[u, n, at, :]
    far_rest = lambda u, at: pkb[u, at, :]
    for c in c_on:
        c.wait()
    c_f = []
    for g in range(Q // CHUNK + 1):
        if g < Q // CHUNK:
            at = pl.ds(g * part, part)
            c_b[g].wait()
            c_f.append(copy(pkb.at[0, at], pkb.at[1, at], 19 + g, sib))
            c_f[g].start()
        if g > 0:
            c_f[g - 1].wait()
            for q in range((g - 1) * CHUNK, g * CHUNK, 2 * PH):
                unpack(q, PH, sel_far, far_early, far_rest, KB, (par_at, dia_at), 1 - a // 2)


def run(n, a_blocks, p_blocks, columns, agg_ids):
    KB, PH = CLASSES[n]
    KL = 2 * KB
    vm = pltpu.VMEM
    up = lambda x: -(-x // 128) * 128
    out = pl.pallas_call(
        functools.partial(kernel, KB, PH),
        out_shape=jax.ShapeDtypeStruct((BAND, 4 * ROWS, BS * BS), BF16),
        in_specs=[pl.BlockSpec(memory_space=pl.ANY)] * 4,
        out_specs=pl.BlockSpec(memory_space=pltpu.VMEM),
        scratch_shapes=[
            pltpu.SMEM((NB,), I32),
            pltpu.SMEM((NNZB, ROWS), I32),
            vm((NNZB, ROWS, BS * BS), BF16),
            vm((ROWS, BS * BS), BF16),
            vm((Q * ROWS, 128), F32),
            vm((ROWS * Q, 128), BF16),
            vm((REACH * Q, 128), BF16),
            vm((REACH * Q, 128), BF16),
            vm((ROWS + 2 * REACH, 128, 128), BF16),
            vm((ROWS * 64, 64), BF16),
            vm((NNZB * Q * ROWS, 128), F32),
            vm((ROWS, 64, 512), BF16),
            vm((ROWS * 8 + 1, Q, 128), F32),
            vm((BAND * Q, 128), BF16),
            vm((BAND * Q, 128), BF16),
            vm((2, BAND * Q, 128), BF16),
            vm((2, Q * 8, 128), BF16),
            vm((len(PARTS), Q * PARTS[0][0], 128), BF16),
            vm((len(PARTS), Q * PARTS[0][0], 128), BF16),
            vm((2, len(PARTS), Q * PARTS[0][0], 128), BF16),
            vm((Q * KB, 128), BF16),
            vm((2, Q * KB, 128), BF16),
            vm((Q * KL, 128), BF16),
            vm((Q * KL, 128), BF16),
            vm((Q * KL, 128), BF16),
            vm((Q * KL, 128), BF16),
            vm((Q * KL, 128), F32),
            vm((NEAR * 2 * BAND * ROWS, up(2 * NEAR * (EARLY + KL) + 8 * NEAR)), BF16),
            vm((PH * 2 * BAND * ROWS, up(2 * PH * (EARLY + KB) + 8 * PH)), BF16),
            pltpu.SMEM((8, 32), I32),
            pltpu.SMEM((EARLY + KL,), I32),
            pltpu.SemaphoreType.DMA((4,)),
            pltpu.SemaphoreType.DMA((27,)),
            pltpu.SemaphoreType.DMA((27,)),
        ],
        compiler_params=pltpu.CompilerParams(collective_id=n, has_side_effects=True, vmem_limit_bytes=48 << 20),
    )(agg_ids, columns.T, jnp.transpose(a_blocks, (1, 0, 2)), p_blocks)
    return jnp.transpose(out, (1, 0, 2))


def local(a_blocks, p_blocks, columns, agg_ids):
    which = pl.pallas_call(
        choose,
        out_shape=jax.ShapeDtypeStruct((1,), I32),
        in_specs=[pl.BlockSpec(memory_space=pltpu.VMEM)],
        out_specs=pl.BlockSpec(memory_space=pltpu.SMEM),
    )(agg_ids.reshape(Q, 128))
    branches = [functools.partial(run, n) for n in range(len(CLASSES))]
    return lax.switch(which[0], branches, a_blocks, p_blocks, columns, agg_ids)


def solution(mesh):
    return jax.shard_map(
        local,
        mesh=mesh,
        in_specs=(
            P(("tile", "agg"), None, None),
            P(("tile", "agg"), None),
            P(("tile", "agg"), None),
            P(),
        ),
        out_specs=P("tile", None, None),
        check_vma=False,
    )
```

```python
import functools

import jax
import jax.numpy as jnp
from jax import lax
from jax.experimental import pallas as pl
from jax.experimental.pallas import tpu as pltpu
from jax.sharding import PartitionSpec as P

MESH = pl.DeviceIdType.MESH
BS = 64
NNZB = 6
REACH = 3
BAND = 7
ROWS = 16
NB = 4096
Q = 32
CHUNK = 8
PARTS = ((8, 1), (8, 2), (8, 3))
EARLY = sum(f for f, _ in PARTS)
LAST = 9
NEAR = 2
CLASSES = ((16, 2), (24, 2), (112, 2))
F32 = jnp.float32
BF16 = jnp.bfloat16
I32 = jnp.int32


def dot(x, y):
    return lax.dot_general(x, y, (((1,), (0,)), ((), ())), preferred_element_type=F32)


def dot_nt(x, y):
    return lax.dot_general(x, y, (((1,), (1,)), ((), ())), preferred_element_type=F32)


def iota(shape, dim):
    return lax.broadcasted_iota(I32, shape, dim)


def level(place, length):
    end = place + length - 1
    soon = jnp.logical_and(place >= REACH, end <= LAST)
    return jnp.where(soon, 1, jnp.where(end < ROWS - REACH, 2, 3))


def choose(ids_ref, out_ref):
    ids = ids_ref[...]
    row, lane = iota((Q, 128), 0), iota((Q, 128), 1)
    flat = row * 128 + lane
    final = jnp.max(ids)

    def at(step):
        moved = pltpu.roll(ids, (-step) % 128, 1)
        other = pltpu.roll(moved, (Q - 1) if step > 0 else 1, 0)
        inside = lane + step < 128 if step > 0 else lane + step >= 0
        got = jnp.where(inside, moved, other)
        return jnp.where(flat + step >= NB, final, jnp.where(flat + step < 0, 0, got))

    start = jnp.logical_or(flat == 0, at(-1) != ids)
    high = at(6)
    length = jnp.full((Q, 128), 4, I32)
    for n in (3, 2, 1):
        ends = jnp.logical_or(at(n) != ids, flat + n >= NB)
        high = jnp.where(ends, at(n - 1 + REACH), high)
        length = jnp.where(ends, n, length)
    count = jnp.where(start, high - at(-REACH) + 1, 0)
    place = lax.rem(lane, ROWS)
    grade = level(place, length)
    sums = (iota((128, 128), 0) // ROWS == iota((128, 128), 1)).astype(F32).astype(BF16)
    upto = [jnp.where(grade <= most, count, 0).astype(F32).astype(BF16) for _, most in PARTS]
    upto = dot(jnp.concatenate(upto + [count.astype(F32).astype(BF16)], axis=0), sums)
    used = 0.0
    for n, (slots, _) in enumerate(PARTS):
        used = used + jnp.minimum(upto[n * Q:(n + 1) * Q] - used, float(slots))
    rest = upto[len(PARTS) * Q:] - used
    pair = jnp.where(lax.rem(lane, 2) == 0, rest + pltpu.roll(rest, 127, 1), 0.0)
    most = jnp.max(pair)
    which = jnp.int32(0)
    for slots, _ in CLASSES[:-1]:
        which = which + (most > float(2 * slots)).astype(I32)
    out_ref[0] = which


def segment(ids, g):
    last = NB - 1
    own = ids[g]
    start = jnp.logical_or(g == 0, ids[jnp.maximum(g - 1, 0)] != own)
    length = jnp.int32(1)
    for step in range(1, 4):
        same = jnp.logical_and(g + step <= last, ids[jnp.minimum(g + step, last)] == own)
        length = length + same.astype(I32)
    low = ids[jnp.maximum(g - REACH, 0)] - own + REACH
    high = ids[jnp.minimum(g + length - 1 + REACH, last)] - own + REACH
    return start, low, high, length


def parts_of(upto):
    ends, used = [], 0
    for n, (slots, _) in enumerate(PARTS):
        used = used + jnp.minimum(upto[n] - used, slots)
        ends.append(used)
    return ends


def each(begin, end, body):
    if end - begin <= 64:
        for m in range(begin, end):
            body(m)
    else:
        pl.loop(begin, end)(body)


def kernel(KB, PH, ids_in, cols_in, a_in, p_in, out_ref, ids, cols, a_ref, p_ref, pscr, p2, hl, hr, dmat, lmat, ascr, bscr, blk, lead_out, lead_in, lead_far, lead_rows,
           wa, sib_a, pka, wb, pkb, own_l, own_rows, sib_l, sib_rows, wf, sel_near, sel_far, tab, walk, lsem, ssem, rsem):
    KL = 2 * KB
    t = lax.axis_index("tile")
    a = lax.axis_index("agg")
    rank = t * 4 + a
    base = rank * ROWS
    ranks = NB // ROWS
    nxt = lax.rem(rank + 1, ranks)
    prv = lax.rem(rank + ranks - 1, ranks)
    dev = lambda r: (r // 4, lax.rem(r, 4))
    sib_at = a + 1 - 2 * lax.rem(a, 2)
    par_at = lax.rem(a + 2, 4)
    dia_at = lax.rem(sib_at + 2, 4)
    sib, par = (t, sib_at), (t, par_at)
    bar = pltpu.get_barrier_semaphore()
    for d in (dev(nxt), dev(prv), sib, par):
        pl.semaphore_signal(bar, inc=1, device_id=d, device_id_type=MESH)
    tiles = ranks // 4
    before = lax.rem(t + tiles - 1, tiles)

    @pl.when(a == 0)
    def _():
        for d in (lax.rem(t + 1, tiles), before):
            pl.semaphore_signal(bar, inc=1, device_id=(d, a), device_id_type=MESH)


    def copy(src, dst, n, to):
        return pltpu.make_async_remote_copy(src_ref=src, dst_ref=dst, send_sem=ssem.at[n], recv_sem=rsem.at[n], device_id=to, device_id_type=MESH)

    loads = [pltpu.make_async_copy(x, y, lsem.at[n]) for n, (x, y) in enumerate(((p_in, p_ref), (ids_in, ids), (cols_in, cols), (a_in, a_ref)))]
    for c in loads:
        c.start()
    loads[0].wait()

    pf = p_ref[...].astype(F32)
    for q in range(Q):
        pscr[pl.ds(q * ROWS, ROWS), :] = pf[:, q * 128:(q + 1) * 128]
    for i in range(ROWS):
        p2[pl.ds(i * Q, Q), :] = pscr[pl.ds(i, Q, stride=ROWS), :].astype(BF16)
    H = REACH * Q
    c_right = copy(p2.at[pl.ds((ROWS - REACH) * Q, H)], hl, 0, dev(nxt))
    c_left = copy(p2.at[pl.ds(0, H)], hr, 1, dev(prv))

    def meet():
        pl.semaphore_wait(bar, 4 + 2 * (a == 0).astype(I32))
        c_right.start()
        c_left.start()

    @pl.when(a >= 2)
    def _():
        meet()


    loads[1].wait()

    tab[0, ROWS], tab[1, ROWS], tab[2, ROWS], tab[3, ROWS], tab[4, ROWS] = jnp.int32(0), jnp.int32(1 << 20), jnp.int32(ROWS), jnp.int32(ROWS), jnp.int32(9)
    starts, grades = [], []
    upto = [jnp.int32(0)] * (len(PARTS) + 1)
    for i in range(ROWS):
        start, lo, hi, length = segment(ids, base + i)
        grade = level(i, length)
        starts.append(start)
        grades.append(grade)
        tab[0, i] = lo
        tab[1, i] = hi
        tab[2, i] = jnp.minimum(i + length - 1, ROWS - 1)
        tab[4, i] = grade
        here = jnp.where(start, hi - lo + 1, 0)
        for n in range(len(PARTS) + 1):
            upto[n] = upto[n] + (jnp.where(grade <= PARTS[n][1], here, 0) if n < len(PARTS) else here)
    after = jnp.int32(ROWS)
    link = [None] * ROWS
    for i in range(ROWS - 1, REACH - 1, -1):
        link[i] = after
        after = jnp.where(jnp.logical_and(starts[i], grades[i] > 1), i, after)
    for i in range(REACH - 1, -1, -1):
        link[i] = after
        after = jnp.where(starts[i], i, after)
    for i in range(ROWS - 1, REACH - 1, -1):
        soon = jnp.logical_and(starts[i], grades[i] == 1)
        link[i] = jnp.where(soon, after, link[i])
        after = jnp.where(soon, i, after)
    for i in range(ROWS):
        tab[3, i] = link[i]
    mine_rest = upto[-1] - parts_of(upto)[-1]
    def step(most, m, state):
        s, o = state
        end = tab[2, s]
        fits = tab[4, s] <= most
        walk[m] = jnp.where(fits, jnp.clip(end * 8 + o, 0, ROWS * 8), ROWS * 8)
        more = jnp.logical_or(o < tab[1, s], jnp.logical_not(fits))
        s2 = jnp.where(more, s, tab[3, s])
        return s2, jnp.where(more, o + fits.astype(I32), tab[0, s2])

    state, m = (after, tab[0, after]), 0
    for slots, most in PARTS + ((KL, 99),):
        if slots <= 64:
            for _ in range(slots):
                state = step(most, m, state)
                m += 1
        else:
            state = lax.fori_loop(m, m + slots, functools.partial(step, most), state)

    r_, c_ = iota((128, 64), 0), iota((128, 64), 1)
    cc = lax.rem(r_, 64)
    flip = (lax.rem(cc, 2) != r_ // 64).astype(I32)
    spread = (c_ == cc // 2 + 32 * flip).astype(F32).astype(BF16)
    diag = (iota((128, 128), 0) // 64) == (iota((128, 128), 1) // 64)
    low = iota((Q, 128), 1) < 64

    def spread_block(blockf):
        both = jnp.concatenate([blockf, pltpu.roll(blockf, 64, 1)], axis=0).astype(BF16)
        return jnp.where(diag, dot(spread, both), 0.0).astype(BF16)

    pr, pc = iota((64, 128), 0), iota((64, 128), 1)
    order = jnp.where(pr < 32, 2 * pr, 2 * (pr - 32) + 1)
    perm = (lax.rem(pc, 64) == order).astype(F32).astype(BF16)
    for i in range(ROWS):
        bf = p2[pl.ds(i * Q, Q), :].astype(F32)
        dmat[i + REACH] = spread_block(bf)
        split = jnp.concatenate([jnp.where(low, bf, 0.0), jnp.where(low, 0.0, bf)], axis=0).astype(BF16)
        lmat[pl.ds(i * 64, 64), :] = dot_nt(perm, split).astype(BF16)
    loads[2].wait()
    loads[3].wait()
    for k in range(NNZB):
        x = a_ref[k].astype(F32)
        for q in range(Q):
            ascr[pl.ds(k * 512 + q * ROWS, ROWS), :] = x[:, q * 128:(q + 1) * 128]

    def products(i):
        own = ids[base + i]
        bands = [jnp.zeros((Q, 128), F32)] * 8
        for k in range(NNZB):
            a2 = ascr[pl.ds(k * 512 + i, Q, stride=ROWS), :].astype(BF16)
            j = cols[k, i]
            prod = dot(a2, dmat[jnp.clip(j - base + REACH, 0, ROWS + 2 * REACH - 1)])
            o = ids[j] - own + REACH
            for b in range(BAND):
                bands[b] = bands[b] + jnp.where(o == b, 1.0, 0.0).astype(F32) * prod
        ev, od = [], []
        for m in range(4):
            x0, x1 = bands[2 * m], bands[2 * m + 1]
            ev.append(jnp.where(low, x0, pltpu.roll(x1, 64, 1)))
            od.append(jnp.where(low, pltpu.roll(x0, 64, 1), x1))
        bscr[i] = jnp.concatenate([jnp.concatenate(ev, axis=1), jnp.concatenate(od, axis=1)], axis=0).astype(BF16)

    def row(i, acc):
        term = dot(lmat[pl.ds(i * 64, 64), :], bscr[i])
        if acc is not None:
            term = term + jnp.where(ids[base + i - 1] == ids[base + i], 1.0, 0.0).astype(F32) * acc
        for m in range(4):
            x0, y0 = term[:Q, m * 128:(m + 1) * 128], term[Q:, m * 128:(m + 1) * 128]
            blk[i * 8 + 2 * m] = jnp.where(low, x0, pltpu.roll(y0, 64, 1))
            if m < 3:
                blk[i * 8 + 2 * m + 1] = jnp.where(low, pltpu.roll(x0, 64, 1), y0)
        return term

    def rows(begin, end, acc):
        for i in range(begin, end):
            products(i)
        for i in range(begin, end):
            acc = row(i, acc)
        return acc

    def early(n):
        first = sum(f for f, _ in PARTS[:n])
        slots = PARTS[n][0]
        for m in range(slots):
            wf[pl.ds(m, Q, stride=slots), :] = blk[walk[first + m]]
        wa[n] = wf[pl.ds(0, Q * slots), :].astype(BF16)
        for c in c_early[n]:
            c.start()

    c_early = [(copy(wa.at[n], pka.at[0, n], 6 + 2 * n, par), copy(wa.at[n], sib_a.at[n], 7 + 2 * n, sib)) for n in range(len(PARTS))]

    blk[ROWS * 8] = jnp.zeros((Q, 128), F32)
    acc = rows(REACH, LAST + 1, None)

    @pl.when(a >= 2)
    def _():
        early(0)

    acc = rows(LAST + 1, ROWS - REACH, acc)

    @pl.when(a < 2)
    def _():
        meet()
        early(0)

    c_right.wait()
    c_left.wait()
    for i in range(REACH):
        dmat[i] = spread_block(hl[pl.ds(i * Q, Q), :].astype(F32))
        dmat[i + REACH + ROWS] = spread_block(hr[pl.ds(i * Q, Q), :].astype(F32))
    rows(0, REACH, None)

    leads = jnp.where(jnp.logical_and(base > 0, ids[jnp.maximum(base - 1, 0)] == ids[base]), 1.0, 0.0).astype(F32)
    e, run = jnp.int32(0), jnp.int32(1)
    for step in range(1, REACH):
        run = run * (ids[base + step] == ids[base]).astype(I32)
        e = e + run
    for o in range(BAND):
        lead_out[pl.ds(o * Q, Q), :] = (leads * blk[e * 8 + o]).astype(BF16)
    c_lead = copy(lead_out, lead_in, 2, sib)
    c_lead.start()

    def outer(k):
        to = t if k == 0 else before
        return [pltpu.make_async_remote_copy(src_ref=lead_out, dst_ref=lead_far.at[k], send_sem=ssem.at[23 + n], recv_sem=rsem.at[23 + k], device_id=(to, d), device_id_type=MESH) for n, d in enumerate((0, 3))]

    for k in range(2):
        @pl.when(a == 2 - 2 * k)
        def _(k=k):
            for c in outer(k):
                c.start()

    for i in range(REACH, 2 * REACH):
        joined = jnp.where(ids[base + i] == ids[base + REACH - 1], 1.0, 0.0).astype(F32)
        for o in range(BAND):
            blk[i * 8 + o] = blk[i * 8 + o] + joined * blk[(REACH - 1) * 8 + o]

    early(1)
    rows(ROWS - REACH, ROWS, acc)
    c_lead.wait()
    even = jnp.where(lax.rem(a, 2) == 0, 1.0, 0.0).astype(F32)
    for o in range(BAND):
        at = (ROWS - 1) * 8 + o
        blk[at] = blk[at] + even * lead_in[pl.ds(o * Q, Q), :].astype(F32)
    early(2)
    def keep(m):
        own_l[pl.ds(pl.multiple_of(m * Q, Q), Q), :] = blk[walk[EARLY + m]].astype(BF16)

    each(KB, KL, keep)
    tail, body = pl.ds(KB * Q, KB * Q), pl.ds(0, KB * Q)
    c_tail = copy(own_l.at[tail], sib_l.at[tail], 3, sib)
    c_tail.start()
    each(0, KB, keep)
    c_body = copy(own_l.at[body], sib_l.at[body], 4, sib)
    c_body.start()
    c_tail.wait()

    def share(h):
        v = own_l[pl.ds(pl.multiple_of(h * Q, Q), Q), :].astype(F32)
        v = jnp.where(h < mine_rest, v, sib_l[pl.ds(pl.multiple_of((KL - 1 - h) * Q, Q), Q), :].astype(F32))
        wf[pl.ds(h, Q, stride=KB), :] = v

    each(0, KB, share)
    part = CHUNK * KB
    c_b = []
    for g in range(Q // CHUNK):
        at = pl.ds(g * part, part)
        wb[at, :] = wf[at, :].astype(BF16)
        c_b.append(copy(wb.at[at], pkb.at[0, at], 15 + g, par))
        c_b[-1].start()

    sub, lane = iota((ROWS, 128), 0), iota((ROWS, 128), 1)

    def places(which):
        begin = (t * 4 + which) * ROWS
        zero = jnp.zeros((ROWS, 128), I32)
        shift, lows, highs = zero, zero + 8, zero
        found = [segment(ids, begin + i) for i in range(ROWS)]
        grades = [level(i, found[i][3]) for i in range(ROWS)]
        here = [jnp.where(start, hi - lo + 1, 0) for start, lo, hi, _ in found]
        upto = [sum(jnp.where(grades[i] <= most, here[i], 0) for i in range(ROWS)) for _, most in PARTS] + [sum(here)]
        soon, later = jnp.int32(0), upto[0]
        for i in range(ROWS):
            start, lo, hi, _ = found[i]
            row_i = sub == i
            lows = jnp.where(row_i, jnp.where(start, lo, 8), lows)
            highs = jnp.where(row_i, hi, highs)
            shift = jnp.where(row_i, jnp.where(grades[i] == 1, soon, later) - lo, shift)
            soon = soon + jnp.where(grades[i] == 1, here[i], 0)
            later = later + jnp.where(grades[i] == 1, 0, here[i])
        ends = parts_of(upto)
        final = jnp.int32(0)
        for i in range(ROWS):
            final = jnp.where(found[i][0], i, final)
        final = jnp.where(lax.rem(which, 2) == 1, final, -1)
        return [(jnp.logical_and(lows <= o, highs >= o), shift + o) for o in range(BAND)], ends, final

    def build(sel, P_, pair, last, shared):
        for u, which in enumerate(pair):
            blocks, ends, final = places(which)
            for o, (there, n) in enumerate(blocks):
                m = n - ends[-1]
                if shared:
                    col = jnp.where(m < last, m + u * P_ * last, 2 * last - 1 - m + (1 - u) * P_ * last)
                else:
                    col = m + u * P_ * last
                col = col + 2 * P_ * EARLY
                step = jnp.full((ROWS, 128), last, I32)
                for k in range(len(PARTS) - 1, -1, -1):
                    slots = PARTS[k][0]
                    inside = n < ends[k]
                    begin = ends[k - 1] if k else 0
                    base_col = 2 * P_ * sum(f for f, _ in PARTS[:k]) + u * P_ * slots
                    col = jnp.where(inside, n - begin + base_col, col)
                    step = jnp.where(inside, slots, step)
                col = jnp.where(there, col, -(1 << 20))
                col2 = jnp.where(sub == final, 2 * P_ * (EARLY + last) + o, -(1 << 20))
                for p in range(P_):
                    at = pl.ds(((p * BAND + o) * 2 + u) * ROWS, ROWS)
                    for c in range(sel.shape[1] // 128):
                        sel[at, pl.ds(c * 128, 128)] = jnp.where(jnp.logical_or(col == lane + c * 128, col2 == lane + c * 128), 1.0, 0.0).astype(BF16)
                    col, col2 = col + step, col2 + 8

    def unpack(q, P_, sel, early_of, rest_of, last, where, lead):
        wide = []
        for x in (q, q + P_):
            tall = []
            for n, (slots, _) in enumerate(PARTS):
                tall += [early_of(u, n, pl.ds(x * slots, P_ * slots)) for u in range(2)]
            tall += [rest_of(u, pl.ds(x * last, P_ * last)) for u in range(2)]
            tall.append(lead_rows[lead, pl.ds(x * 8, P_ * 8), :])
            wide.append(jnp.concatenate(tall, axis=0))
        got = dot(sel[:, :2 * P_ * (EARLY + last) + 8 * P_], jnp.concatenate(wide, axis=1)).astype(BF16)
        for p in range(P_):
            for o in range(BAND):
                for u in range(2):
                    at = pl.ds(pl.multiple_of(where[u] * ROWS, ROWS), ROWS)
                    rows = got[((p * BAND + o) * 2 + u) * ROWS:((p * BAND + o) * 2 + u + 1) * ROWS]
                    out_ref[o, at, pl.ds((q + p) * 128, 128)] = rows[:, :128]
                    out_ref[o, at, pl.ds((q + P_ + p) * 128, 128)] = rows[:, 128:]

    build(sel_near, NEAR, (a, sib_at), KL, False)
    def lay(ref, m):
        wf[pl.ds(m, Q, stride=KL), :] = ref[pl.ds(pl.multiple_of(m * Q, Q), Q), :].astype(F32)

    each(0, KL, functools.partial(lay, own_l))
    own_rows[...] = wf[pl.ds(0, Q * KL), :].astype(BF16)
    for _, to_sib in c_early:
        to_sib.wait()
    c_body.wait()
    each(0, KL, functools.partial(lay, sib_l))
    sib_rows[...] = wf[pl.ds(0, Q * KL), :].astype(BF16)
    near_early = lambda u, n, at: (wa, sib_a)[u][n, at, :]
    near_rest = lambda u, at: (own_rows, sib_rows)[u][at, :]
    c_on = []
    for n, (to_par, _) in enumerate(c_early):
        to_par.wait()
        c_on.append(copy(pka.at[0, n], pka.at[1, n], 12 + n, sib))
        c_on[-1].start()
    first_hop = [pltpu.make_async_remote_copy(src_ref=lead_out, dst_ref=lead_far.at[k], send_sem=ssem.at[23], recv_sem=rsem.at[23 + k], device_id=sib, device_id_type=MESH) for k in range(2)]
    second_hop = [copy(lead_far.at[k], lead_far.at[k], 25 + k, sib) for k in range(2)]
    ends_here = jnp.logical_or(a == 0, a == 3)

    @pl.when(ends_here)
    def _():
        for k in range(2):
            first_hop[k].wait_recv()
            second_hop[k].start()
        for k in range(2):
            second_hop[k].wait_send()

    @pl.when(jnp.logical_not(ends_here))
    def _():
        for k in range(2):
            second_hop[k].wait_recv()

    for k in range(2):
        @pl.when(a == 2 - 2 * k)
        def _(k=k):
            for c in outer(k):
                c.wait_send()

    for k in range(2):
        for o in range(BAND):
            wf[pl.ds(o, Q, stride=8), :] = lead_far[k, pl.ds(o * Q, Q), :].astype(F32)
        wf[pl.ds(BAND, Q, stride=8), :] = jnp.zeros((Q, 128), F32)
        lead_rows[k] = wf[pl.ds(0, Q * 8), :].astype(BF16)
    build(sel_far, PH, (par_at, dia_at), KB, True)

    c_f = []
    for g in range(Q // CHUNK):
        for q in range(g * CHUNK, (g + 1) * CHUNK, 2 * NEAR):
            unpack(q, NEAR, sel_near, near_early, near_rest, KL, (a, sib_at), a // 2)
        at = pl.ds(g * part, part)
        c_b[g].wait()
        c_f.append(copy(pkb.at[0, at], pkb.at[1, at], 19 + g, sib))
        c_f[g].start()

    far_early = lambda u, n, at: pka[u, n, at, :]
    far_rest = lambda u, at: pkb[u, at, :]
    for c in c_on:
        c.wait()
    for g in range(Q // CHUNK):
        c_f[g].wait()
        for q in range(g * CHUNK, (g + 1) * CHUNK, 2 * PH):
            unpack(q, PH, sel_far, far_early, far_rest, KB, (par_at, dia_at), 1 - a // 2)


def run(n, a_blocks, p_blocks, columns, agg_ids):
    KB, PH = CLASSES[n]
    KL = 2 * KB
    vm = pltpu.VMEM
    up = lambda x: -(-x // 128) * 128
    out = pl.pallas_call(
        functools.partial(kernel, KB, PH),
        out_shape=jax.ShapeDtypeStruct((BAND, 4 * ROWS, BS * BS), BF16),
        in_specs=[pl.BlockSpec(memory_space=pl.ANY)] * 4,
        out_specs=pl.BlockSpec(memory_space=pltpu.VMEM),
        scratch_shapes=[
            pltpu.SMEM((NB,), I32),
            pltpu.SMEM((NNZB, ROWS), I32),
            vm((NNZB, ROWS, BS * BS), BF16),
            vm((ROWS, BS * BS), BF16),
            vm((Q * ROWS, 128), F32),
            vm((ROWS * Q, 128), BF16),
            vm((REACH * Q, 128), BF16),
            vm((REACH * Q, 128), BF16),
            vm((ROWS + 2 * REACH, 128, 128), BF16),
            vm((ROWS * 64, 64), BF16),
            vm((NNZB * Q * ROWS, 128), F32),
            vm((ROWS, 64, 512), BF16),
            vm((ROWS * 8 + 1, Q, 128), F32),
            vm((BAND * Q, 128), BF16),
            vm((BAND * Q, 128), BF16),
            vm((2, BAND * Q, 128), BF16),
            vm((2, Q * 8, 128), BF16),
            vm((len(PARTS), Q * PARTS[0][0], 128), BF16),
            vm((len(PARTS), Q * PARTS[0][0], 128), BF16),
            vm((2, len(PARTS), Q * PARTS[0][0], 128), BF16),
            vm((Q * KB, 128), BF16),
            vm((2, Q * KB, 128), BF16),
            vm((Q * KL, 128), BF16),
            vm((Q * KL, 128), BF16),
            vm((Q * KL, 128), BF16),
            vm((Q * KL, 128), BF16),
            vm((Q * KL, 128), F32),
            vm((NEAR * 2 * BAND * ROWS, up(2 * NEAR * (EARLY + KL) + 8 * NEAR)), BF16),
            vm((PH * 2 * BAND * ROWS, up(2 * PH * (EARLY + KB) + 8 * PH)), BF16),
            pltpu.SMEM((8, 32), I32),
            pltpu.SMEM((EARLY + KL,), I32),
            pltpu.SemaphoreType.DMA((4,)),
            pltpu.SemaphoreType.DMA((27,)),
            pltpu.SemaphoreType.DMA((27,)),
        ],
        compiler_params=pltpu.CompilerParams(collective_id=n, has_side_effects=True, vmem_limit_bytes=48 << 20),
    )(agg_ids, columns.T, jnp.transpose(a_blocks, (1, 0, 2)), p_blocks)
    return jnp.transpose(out, (1, 0, 2))


def local(a_blocks, p_blocks, columns, agg_ids):
    which = pl.pallas_call(
        choose,
        out_shape=jax.ShapeDtypeStruct((1,), I32),
        in_specs=[pl.BlockSpec(memory_space=pltpu.VMEM)],
        out_specs=pl.BlockSpec(memory_space=pltpu.SMEM),
    )(agg_ids.reshape(Q, 128))
    branches = [functools.partial(run, n) for n in range(len(CLASSES))]
    return lax.switch(which[0], branches, a_blocks, p_blocks, columns, agg_ids)


def solution(mesh):
    return jax.shard_map(
        local,
        mesh=mesh,
        in_specs=(
            P(("tile", "agg"), None, None),
            P(("tile", "agg"), None),
            P(("tile", "agg"), None),
            P(),
        ),
        out_specs=P("tile", None, None),
        check_vma=False,
    )
```
